32 devices in a mesh: clip: 4 (over z), vid: 4 (over y, core), aud: 2 (over x).
Axes of the slice: x: 2, y: 2, z: 4, core: 2. Of those that a mesh axis runs over, the one named last changes fastest.
Arguments:
- video_tokens: bfloat16 [4, 512, 2048], P('clip', 'vid'), may hold values from -6 to 6
- audio_tokens: bfloat16 [4, 512, 2048], P('clip', 'vid'), may hold values from -6 to 6
- qkv_video: bfloat16 [2048, 16, 384], P(None, 'aud'), may hold values from -0.125 to 0.125
- out_video: bfloat16 [16, 128, 2048], P('aud'), may hold values from -0.125 to 0.125
- qkv_audio: bfloat16 [2048, 16, 384], P(None, 'aud'), may hold values from -0.125 to 0.125
- out_audio: bfloat16 [16, 128, 2048], P('aud'), may hold values from -0.125 to 0.125
- gain_video: float32 [2048], replicated, may hold values from 0.5 to 1.5
- gain_audio: float32 [2048], replicated, may hold values from 0.5 to 1.5
- time_from: float32 [65, 2048], replicated, may hold values from -1.8 to 1.8
- time_to: float32 [65, 2048], replicated, may hold values from -1.8 to 1.8
- time_steps: int32 [4, 2], P('clip'), may hold values from 0 to 64, as said below
- windows: int32 [4, 2], P('clip'), may hold values from 32 to 128
- intersection: int32 [4, 16, 2], P('clip'), may hold values from 0 to 16, as said below
Outputs:
- d_video: bfloat16 [4, 512, 2048], P('clip', 'vid')
- d_audio: bfloat16 [4, 512, 2048], P('clip', 'vid')
- grad_qkv_video: float32 [2048, 16, 384], P(('clip', 'vid'), 'aud')
- grad_out_video: float32 [16, 128, 2048], P('aud', None, ('clip', 'vid'))
- grad_qkv_audio: float32 [2048, 16, 384], P(('clip', 'vid'), 'aud')
- grad_out_audio: float32 [16, 128, 2048], P('aud', None, ('clip', 'vid'))
The draws below stay inside these ranges and needn't reach their ends.
Inputs may be any that keep to these rules, and one draw needn't show every extreme that they name: `time_steps`: column 1 (m) is 1 or more and 2 * m <= column 0 (t) <= 64. `intersection`: entry b holds (lo, hi) with lo < hi, max(b * 32 - 128, 0) <= lo * 32 <= b * 32 and (hi - lo) * 32 <= 160.
All inputs are finite; a program needn't handle non-finite values.
Results may differ from the reference program's by a relative error of at most 0.029.
Values may be sent and summed in bfloat16 or wider, within the bound.
No kernel may reach another device: no remote copies, remote signals or barrier semaphores. Data moves between devices by JAX's collectives and lax.ppermute only.
A program may use at most 128 MiB of HBM per device.

```python
import jax
import jax.numpy as jnp
from jax import lax

D = 2048
H = 16
DH = 128
TOK_DEV = 128
BLK = 32
TGRID = 64
STEPS = 2
NTOK = 512
CLIPS = 4
NBLK = 16
N_VID = 4
N_AUD = 2


def draw_time_steps(key, part):
    first_key, second_key = jax.random.split(jax.random.fold_in(key, 11))
    stride = jax.random.randint(first_key, (CLIPS,), 1, TGRID // STEPS + 1)
    leeway = TGRID - STEPS * stride
    extra = jax.random.randint(second_key, (CLIPS,), 0, leeway + 1)
    return jnp.stack([STEPS * stride + extra, stride], 1).astype(jnp.int32)


def draw_intersection(key, part):
    per_shard = TOK_DEV // BLK
    first_key, second_key = jax.random.split(jax.random.fold_in(key, 23))
    home = jnp.arange(NBLK, dtype=jnp.int32)
    backward = jax.random.randint(first_key, (CLIPS, NBLK), 0, per_shard + 1)
    counts = jax.random.randint(second_key, (CLIPS, NBLK), 1, per_shard + 2)
    low_block = jnp.maximum(home[None, :] - backward, 0)
    high_block = jnp.minimum(low_block + counts, NBLK)
    return jnp.stack([low_block, high_block], -1).astype(jnp.int32)


def plant(drawn, rng, least, largest):
    shape = drawn.shape
    spot = [jax.random.randint(jax.random.fold_in(rng, axis), (), 0, shape[axis]) for axis in range(len(shape))]
    drawn = drawn.at[tuple(spot)].set(least)
    longest = shape.index(max(shape))
    spot[longest] = (spot[longest] + 1) % shape[longest]
    return drawn.at[tuple(spot)].set(largest)


def shard_levels(own_key, shape, cuts, smallest, high):
    loudness = 1.0
    for dim, parts in cuts:
        steps = jax.random.uniform(jax.random.fold_in(jax.random.fold_in(own_key, 6), dim), (parts,), jnp.float32, smallest / len(cuts), high / len(cuts))
        loudness = loudness * jnp.repeat(jnp.exp(steps), shape[dim] // parts).reshape((-1,) + (1,) * (len(shape) - 1 - dim))
    return loudness


def normal_values(own_key, dims, width, reach, cuts=(), kind=jnp.bfloat16):
    entries = width * jax.random.normal(own_key, dims, jnp.float32)
    if cuts:
        entries = entries * shard_levels(own_key, dims, cuts, -0.22, 0.18)
    return jnp.clip(entries, -reach, reach).astype(kind)


def setup_inputs(seed: int = 0) -> dict:
    splits = jax.random.split(jax.random.key(seed), 14)
    return {
        "video_tokens": normal_values(splits[0], (CLIPS, NTOK, D), 1.0, 6.0, ((0, 4), (1, 4))),
        "audio_tokens": normal_values(splits[1], (CLIPS, NTOK, D), 1.0, 6.0, ((0, 4), (1, 4))),
        "qkv_video": normal_values(splits[2], (D, H, 3 * DH), D ** -0.5, 0.125, ((1, 2),)),
        "out_video": normal_values(splits[3], (H, DH, D), (H * DH) ** -0.5, 0.125, ((0, 2),)),
        "qkv_audio": normal_values(splits[4], (D, H, 3 * DH), D ** -0.5, 0.125, ((1, 2),)),
        "out_audio": normal_values(splits[5], (H, DH, D), (H * DH) ** -0.5, 0.125, ((0, 2),)),
        "gain_video": jnp.clip(1.0 + 0.1 * jax.random.normal(splits[6], (D,), jnp.float32), 0.5, 1.5),
        "gain_audio": jnp.clip(1.0 + 0.1 * jax.random.normal(splits[7], (D,), jnp.float32), 0.5, 1.5),
        "time_from": normal_values(splits[8], (TGRID + 1, D), 0.3, 1.8, (), jnp.float32),
        "time_to": normal_values(splits[9], (TGRID + 1, D), 0.3, 1.8, (), jnp.float32),
        "time_steps": draw_time_steps(jax.random.fold_in(splits[13], 71), 0),
        "windows": plant(jax.random.randint(splits[11], (CLIPS, 2), TOK_DEV // 4, TOK_DEV + 1), jax.random.fold_in(splits[11], 1), TOK_DEV // 4, TOK_DEV).astype(jnp.int32),
        "intersection": draw_intersection(jax.random.fold_in(splits[13], 71), 0),
    }


EPSILON = 1e-06
PRECISE = lax.Precision.HIGHEST

def lookup(time_table, time_index):
    onehot = (jnp.arange(time_table.shape[0], dtype=jnp.int32) == time_index).astype(jnp.float32)
    return jnp.dot(onehot, time_table, precision=PRECISE)

def project_in(current, norm_gain, condition, weight):
    inv_rms = lax.rsqrt(lax.optimization_barrier(jnp.mean(current * current, -1, keepdims=True)) + EPSILON)
    modulation = norm_gain * (1.0 + condition)
    normed = (current * inv_rms * modulation).astype(jnp.bfloat16)
    qkv_rows = jnp.einsum('nd,dhe->nhe', normed.astype(jnp.float32), weight.astype(jnp.float32)).astype(jnp.bfloat16)
    return (normed, inv_rms, modulation, qkv_rows)

def attend(queries, key_rows, value_rows, key_mask):
    factor = DH ** (-0.5)
    scores = jnp.einsum('nhe,lhe->hnl', queries.astype(jnp.float32), key_rows.astype(jnp.float32)) * factor
    scores = jnp.where(key_mask[None], scores, -1e+30)
    shifted = jnp.exp(scores - lax.optimization_barrier(jnp.max(scores, -1, keepdims=True)))
    attn_prob = shifted / lax.optimization_barrier(jnp.sum(shifted, -1, keepdims=True))
    rounded = lax.optimization_barrier(attn_prob.astype(jnp.bfloat16))
    result = jnp.einsum('hnl,lhe->nhe', rounded.astype(jnp.float32), value_rows.astype(jnp.float32)).astype(jnp.bfloat16)
    return (result, attn_prob, rounded)

def attend_back(queries, key_rows, value_rows, attn_prob, rounded, grad_out):
    factor = DH ** (-0.5)
    grad_prob = jnp.einsum('nhe,lhe->hnl', grad_out.astype(jnp.float32), value_rows.astype(jnp.float32))
    center = lax.optimization_barrier(jnp.sum(attn_prob * grad_prob, -1, keepdims=True))
    dscore = lax.optimization_barrier((attn_prob * (grad_prob - center) * factor).astype(jnp.bfloat16))
    dscore_wide = dscore.astype(jnp.float32)
    dquery = jnp.einsum('hnl,lhe->nhe', dscore_wide, key_rows.astype(jnp.float32))
    key_grad = jnp.einsum('hnl,nhe->lhe', dscore_wide, queries.astype(jnp.float32))
    value_grad = jnp.einsum('hnl,nhe->lhe', rounded.astype(jnp.float32), grad_out.astype(jnp.float32))
    return (dquery, key_grad, value_grad)

def grouped_out(heads_out, weight):
    per_group = H // N_AUD
    partial_value = jnp.einsum('ngpe,gpef->gnf', heads_out.reshape(NTOK, N_AUD, per_group, DH).astype(jnp.float32), weight.reshape(N_AUD, per_group, DH, D).astype(jnp.float32))
    partial_value = lax.optimization_barrier(partial_value.astype(jnp.bfloat16))
    return lax.optimization_barrier(jnp.sum(partial_value.astype(jnp.float32), 0))

def grouped_back(grad_rows, weight):
    per_group = H // N_AUD
    partial_value = jnp.einsum('ngpe,dgpe->gnd', grad_rows.reshape(NTOK, N_AUD, per_group, 3 * DH).astype(jnp.float32), weight.reshape(D, N_AUD, per_group, 3 * DH).astype(jnp.float32))
    partial_value = lax.optimization_barrier(partial_value.astype(jnp.bfloat16))
    return lax.optimization_barrier(jnp.sum(partial_value.astype(jnp.float32), 0))

def norm_back(current, inv_rms, modulation, grad_normed):
    scaled = grad_normed * modulation
    return inv_rms * scaled - current * inv_rms ** 3 * lax.optimization_barrier(jnp.mean(scaled * current, -1, keepdims=True))

def blocked(pattern, left_side, right_side, out_shape):
    left_blocks = left_side.reshape((N_VID, TOK_DEV) + left_side.shape[1:])
    right_blocks = right_side.reshape((N_VID, TOK_DEV) + right_side.shape[1:])

    def accumulate(running, block_pair):
        partial_value = jnp.einsum(pattern, block_pair[0].astype(jnp.float32), block_pair[1].astype(jnp.float32))
        partial_value = lax.optimization_barrier(partial_value.astype(jnp.bfloat16)).astype(jnp.float32)
        return (running + partial_value, None)
    summed, unused = lax.scan(accumulate, jnp.zeros(out_shape, jnp.float32), (left_blocks, right_blocks))
    return summed

def build_masks(windows, intersection):
    position = jnp.arange(NTOK, dtype=jnp.int32)
    blocks = position // BLK
    distance = jnp.abs(position[:, None] - position[None, :])
    low_block = intersection[:, 0][blocks]
    high_block = intersection[:, 1][blocks]
    video_cross = (blocks[None, :] >= low_block[:, None]) & (blocks[None, :] < high_block[:, None])
    mask_video = jnp.concatenate([distance < windows[0], video_cross], 1)
    mask_audio = jnp.concatenate([video_cross.T, distance < windows[1]], 1)
    return (mask_video, mask_audio)

def network(video_now, audio_now, condition, key_masks, params):
    qkv_video, out_video, qkv_audio, out_audio, gain_video, gain_audio = params
    video_norm, video_inv, video_mod, video_rows = project_in(video_now, gain_video, condition, qkv_video)
    audio_norm, audio_inv, audio_mod, audio_rows = project_in(audio_now, gain_audio, condition, qkv_audio)
    key_rows = jnp.concatenate([video_rows[:, :, DH:2 * DH], audio_rows[:, :, DH:2 * DH]], 0)
    value_rows = jnp.concatenate([video_rows[:, :, 2 * DH:], audio_rows[:, :, 2 * DH:]], 0)
    video_out, video_prob, video_round = attend(video_rows[:, :, :DH], key_rows, value_rows, key_masks[0])
    audio_out, audio_prob, audio_round = attend(audio_rows[:, :, :DH], key_rows, value_rows, key_masks[1])
    video_field = grouped_out(video_out, out_video)
    audio_field = grouped_out(audio_out, out_audio)
    saved = (video_norm, video_inv, video_mod, video_rows, audio_norm, audio_inv, audio_mod, audio_rows, key_rows, value_rows, video_out, video_prob, video_round, audio_out, audio_prob, audio_round)
    return (video_field, audio_field, saved)

def one_clip(inputs, params, tables):
    video_tokens, audio_tokens, time_steps, windows, intersection = inputs
    qkv_video, out_video, qkv_audio, out_audio, gain_video, gain_audio = params
    time_from, time_to = tables
    key_masks = build_masks(windows, intersection)
    start_video = video_tokens.astype(jnp.float32)
    start_audio = audio_tokens.astype(jnp.float32)
    time_now = time_steps[0]
    stride = time_steps[1]
    euler_step = -stride.astype(jnp.float32) / TGRID
    video_now, audio_now = (start_video, start_audio)
    for teacher_step in range(STEPS):
        time_level = time_now - teacher_step * stride
        condition = lookup(time_from, time_level) + lookup(time_to, time_level)
        video_field, audio_field, unused = network(video_now, audio_now, condition, key_masks, params)
        video_now = video_now + euler_step * video_field
        audio_now = audio_now + euler_step * audio_field
    condition = lookup(time_from, time_now) + lookup(time_to, time_now - STEPS * stride)
    video_field, audio_field, saved = network(start_video, start_audio, condition, key_masks, params)
    video_norm, video_inv, video_mod, video_rows, audio_norm, audio_inv, audio_mod, audio_rows, key_rows, value_rows, video_out, video_prob, video_round, audio_out, audio_prob, audio_round = saved
    span_time = -(STEPS * stride).astype(jnp.float32) / TGRID
    video_diff = start_video + span_time * video_field - video_now
    audio_diff = start_audio + span_time * audio_field - audio_now
    video_grad = (span_time * video_diff).astype(jnp.bfloat16)
    audio_grad = (span_time * audio_diff).astype(jnp.bfloat16)
    video_dout = jnp.einsum('nf,hef->nhe', video_grad.astype(jnp.float32), out_video.astype(jnp.float32)).astype(jnp.bfloat16)
    audio_dout = jnp.einsum('nf,hef->nhe', audio_grad.astype(jnp.float32), out_audio.astype(jnp.float32)).astype(jnp.bfloat16)
    video_dq, video_dk, video_dv = attend_back(video_rows[:, :, :DH], key_rows, value_rows, video_prob, video_round, video_dout)
    audio_dq, audio_dk, audio_dv = attend_back(audio_rows[:, :, :DH], key_rows, value_rows, audio_prob, audio_round, audio_dout)
    key_grad = video_dk + audio_dk
    value_grad = video_dv + audio_dv
    video_dqkv = jnp.concatenate([video_dq, key_grad[:NTOK], value_grad[:NTOK]], -1).astype(jnp.bfloat16)
    audio_dqkv = jnp.concatenate([audio_dq, key_grad[NTOK:], value_grad[NTOK:]], -1).astype(jnp.bfloat16)
    video_back = grouped_back(video_dqkv, qkv_video)
    audio_back = grouped_back(audio_dqkv, qkv_audio)
    d_video = (video_diff + norm_back(start_video, video_inv, video_mod, video_back)).astype(jnp.bfloat16)
    d_audio = (audio_diff + norm_back(start_audio, audio_inv, audio_mod, audio_back)).astype(jnp.bfloat16)
    video_wqkv = blocked('nd,nhe->dhe', video_norm, video_dqkv, (D, H, 3 * DH))
    video_wout = blocked('nhe,nf->hef', video_out, video_grad, (H, DH, D))
    audio_wqkv = blocked('nd,nhe->dhe', audio_norm, audio_dqkv, (D, H, 3 * DH))
    audio_wout = blocked('nhe,nf->hef', audio_out, audio_grad, (H, DH, D))
    return (d_video, d_audio, video_wqkv, video_wout, audio_wqkv, audio_wout)

def reference(video_tokens, audio_tokens, qkv_video, out_video, qkv_audio, out_audio, gain_video, gain_audio, time_from, time_to, time_steps, windows, intersection):
    params = (qkv_video, out_video, qkv_audio, out_audio, gain_video, gain_audio)

    def per_clip(inputs):
        return one_clip(inputs, params, (time_from, time_to))
    results = lax.map(per_clip, (video_tokens, audio_tokens, time_steps, windows, intersection))
    return (results[0], results[1], lax.optimization_barrier(jnp.sum(results[2], 0)), lax.optimization_barrier(jnp.sum(results[3], 0)), lax.optimization_barrier(jnp.sum(results[4], 0)), lax.optimization_barrier(jnp.sum(results[5], 0)))
```

```python
import functools

import jax
import jax.numpy as jnp
from jax import lax
from jax.experimental import pallas as pl
from jax.experimental.pallas import tpu as pltpu
from jax.sharding import PartitionSpec as P

BLK = 32
TGRID = 64
STEPS = 2
EPSILON = 1e-06
MASKED = -1e30
F32 = jnp.float32
BF16 = jnp.bfloat16
NT = (((1,), (1,)), ((), ()))
TN = (((0,), (0,)), ((), ()))


def swap(block, axis, bit):
    count = lax.axis_size(axis)
    return lax.ppermute(block, axis, [(i, i ^ (1 << bit)) for i in range(count)])


def shift(block, axis, distance):
    count = lax.axis_size(axis)
    route = [(i, i + distance) for i in range(count) if 0 <= i + distance < count]
    return lax.ppermute(block, axis, route)


def bits_of(count):
    return count.bit_length() - 1


def gather_steps():
    steps = [("clip", 0)] if lax.axis_size("clip") > 1 else []
    return steps + [("vid", bit) for bit in reversed(range(bits_of(lax.axis_size("vid"))))]


def gather_tokens(block):
    gathered = block[None]
    for axis, bit in gather_steps():
        gathered = jnp.concatenate([gathered, swap(gathered, axis, bit)], 0)
    return gathered


def split_columns(block):
    m, n, width = block.shape
    steps = gather_steps()
    devices = lax.axis_size("clip") * lax.axis_size("vid")
    late = devices >> len(steps)
    parts = block.reshape(m, n, devices, width // devices).transpose(2, 0, 1, 3)
    return parts.reshape((late,) + (2,) * len(steps) + parts.shape[1:])


def scatter_columns(block):
    parts = split_columns(block)[None]
    for axis, bit in gather_steps():
        mine = (lax.axis_index(axis) >> bit) & 1
        keep = lax.dynamic_index_in_dim(parts, mine, 2, keepdims=False)
        send = lax.dynamic_index_in_dim(parts, 1 - mine, 2, keepdims=False)
        parts = jnp.concatenate([keep, swap(send, axis, bit)], 0)
    return parts


def reduce_late(partial):
    for bit in reversed(range(1, bits_of(lax.axis_size("clip")))):
        partial = partial.reshape((2, partial.shape[0] // 2) + partial.shape[1:])
        mine = (lax.axis_index("clip") >> bit) & 1
        keep = lax.dynamic_index_in_dim(partial, mine, 0, keepdims=False)
        send = lax.dynamic_index_in_dim(partial, 1 - mine, 0, keepdims=False)
        partial = keep + swap(send.astype(BF16), "clip", bit).astype(F32)
    return partial[0]


def sum_groups(partial):
    count = lax.axis_size("aud")
    total = partial.astype(F32)
    for step in range(1, count):
        total = total + lax.ppermute(
            partial, "aud", [(i, i ^ step) for i in range(count)]
        ).astype(F32)
    return total


def prepare_kernel(
    steps, place, windows, lists, time_from, time_to, gain_v, gain_a, bias, mods, *, tokens
):
    time_now, stride = steps[0], steps[1]
    levels = [(time_now, time_now), (time_now - stride, time_now - stride)]
    levels.append((time_now, time_now - STEPS * stride))
    for row, (start, end) in enumerate(levels):
        condition = time_from[pl.ds(start, 1), :] + time_to[pl.ds(end, 1), :]
        mods[2 * row : 2 * row + 1, :] = gain_v[...] * (1.0 + condition)
        mods[2 * row + 1 : 2 * row + 2, :] = gain_a[...] * (1.0 + condition)

    device = place[0]
    blocks = tokens // BLK
    all_blocks = place[1]
    shape = (tokens, 3 * tokens)
    row_pos = device * tokens + lax.broadcasted_iota(jnp.int32, shape, 0)
    column = lax.broadcasted_iota(jnp.int32, shape, 1)
    column_pos = (device - 1) * tokens + column
    inside = (column_pos >= 0) & (column_pos < all_blocks * BLK)
    distance = jnp.abs(row_pos - column_pos)
    row_blk = device * blocks + lax.broadcasted_iota(jnp.int32, shape, 0) // BLK
    column_blk = (device - 1) * blocks + column // BLK

    def fill(admitted, part, side):
        bias[part, :, side * 3 * tokens : (side + 1) * 3 * tokens] = jnp.where(
            admitted, 0.0, MASKED
        ).astype(F32)

    fill(inside & (distance < windows[0]), 0, 0)
    fill(inside & (distance < windows[1]), 1, 1)
    low = jnp.zeros(shape, jnp.int32)
    high = jnp.zeros(shape, jnp.int32)
    for block in range(blocks):
        here = row_blk == device * blocks + block
        low = jnp.where(here, lists[device * blocks + block, 0], low)
        high = jnp.where(here, lists[device * blocks + block, 1], high)
    fill(inside & (column_blk >= low) & (column_blk < high), 0, 1)
    low = jnp.zeros(shape, jnp.int32)
    high = jnp.zeros(shape, jnp.int32)
    for block in range(3 * blocks):
        index = (device - 1) * blocks + block
        safe = jnp.clip(index, 0, all_blocks - 1)
        here = column_blk == index
        low = jnp.where(here, lists[safe, 0], low)
        high = jnp.where(here, lists[safe, 1], high)
    fill(inside & (row_blk >= low) & (row_blk < high), 1, 0)


def prepare(time_steps, windows, intersection, time_from, time_to, gain_video, gain_audio, tokens):
    place = jnp.stack([lax.axis_index("vid"), lax.axis_size("vid") * tokens // BLK])
    smem = pl.BlockSpec(memory_space=pltpu.SMEM)
    vmem = pl.BlockSpec(memory_space=pltpu.VMEM)
    width = gain_video.shape[0]
    return pl.pallas_call(
        functools.partial(prepare_kernel, tokens=tokens),
        out_shape=(
            jax.ShapeDtypeStruct((2, tokens, 6 * tokens), F32),
            jax.ShapeDtypeStruct((6, width), F32),
        ),
        in_specs=[smem] * 4 + [vmem] * 4,
        out_specs=(vmem, vmem),
        name="prepare",
    )(
        time_steps[0],
        place.astype(jnp.int32),
        windows[0],
        intersection[0],
        time_from,
        time_to,
        gain_video[None],
        gain_audio[None],
    )


def soft(queries, keys, bias, factor):
    scores = lax.dot_general(queries, keys, NT, preferred_element_type=F32) * factor + bias
    shifted = jnp.exp(scores - jnp.max(scores, -1, keepdims=True))
    return shifted * (1.0 / jnp.sum(shifted, -1, keepdims=True))


def key_values(head, rows_v, left_v, right_v, rows_a, left_a, right_a):
    size = left_v.shape[-1] // 2
    keys, values = [], []
    for left, rows, right in ((left_v, rows_v, right_v), (left_a, rows_a, right_a)):
        keys += [left[head, :, :size], rows[head, :, size : 2 * size], right[head, :, :size]]
        values += [left[head, :, size:], rows[head, :, 2 * size :], right[head, :, size:]]
    return jnp.concatenate(keys, 0), jnp.concatenate(values, 0)


def forward_kernel(
    rows_v, left_v, right_v, rows_a, left_a, right_a, bias, w_out, heads_out, field, total, *, part
):
    step = pl.program_id(0)
    group, tokens, size = heads_out.shape
    own = (rows_v, rows_a)[part]
    outs = []
    for head in range(group):
        keys, values = key_values(head, rows_v, left_v, right_v, rows_a, left_a, right_a)
        prob = soft(own[head, :, :size], keys, bias[0], size**-0.5)
        out = jnp.dot(prob.astype(BF16), values, preferred_element_type=F32).astype(BF16)
        heads_out[head] = out
        outs.append(out)
    term = jnp.dot(
        jnp.concatenate(outs, 1),
        w_out[...].reshape(group * size, w_out.shape[-1]),
        preferred_element_type=F32,
    )

    @pl.when(step == 0)
    def _():
        total[...] = term

    @pl.when(step > 0)
    def _():
        total[...] += term

    @pl.when(step == pl.num_programs(0) - 1)
    def _():
        field[...] = total[...].astype(BF16)


def head_block(group, array):
    return pl.BlockSpec((group,) + array.shape[1:], lambda i: (i, 0, 0))


def attend(keys, bias, w_out, part):
    heads, size, width = w_out.shape
    tokens = keys[0].shape[1]
    group = 2 if heads % 2 == 0 else 1
    flops = 2 * heads * tokens * size * (12 * tokens + width)
    return pl.pallas_call(
        functools.partial(forward_kernel, part=part),
        grid=(heads // group,),
        out_shape=(
            jax.ShapeDtypeStruct((heads, tokens, size), BF16),
            jax.ShapeDtypeStruct((tokens, width), BF16),
        ),
        in_specs=[head_block(group, array) for array in keys]
        + [
            pl.BlockSpec((1,) + bias.shape[1:], lambda i: (part, 0, 0)),
            head_block(group, w_out),
        ],
        out_specs=(
            pl.BlockSpec((group, tokens, size), lambda i: (i, 0, 0)),
            pl.BlockSpec((tokens, width), lambda i: (0, 0)),
        ),
        scratch_shapes=[pltpu.VMEM((tokens, width), F32)],
        compiler_params=pltpu.CompilerParams(vmem_limit_bytes=24 * 2**20),
        cost_estimate=pl.CostEstimate(
            flops=flops, bytes_accessed=heads * size * width * 2, transcendentals=0
        ),
        name="attend",
    )(*keys, bias, w_out)


def backward_kernel(
    rows_v,
    left_v,
    right_v,
    rows_a,
    left_a,
    right_a,
    bias,
    grad_v,
    grad_a,
    w_out_v,
    w_out_a,
    own_v,
    own_a,
    to_left,
    to_right,
):
    group, tokens, triple = rows_v.shape
    size = triple // 3
    factor = size**-0.5
    both_bias = bias[...].reshape(2 * tokens, 6 * tokens)
    width = w_out_v.shape[-1]
    grads_out = [
        lax.dot_general(
            grad[...], w_out[...].reshape(group * size, width), NT, preferred_element_type=F32
        ).astype(BF16)
        for grad, w_out in ((grad_v, w_out_v), (grad_a, w_out_a))
    ]
    for head in range(group):
        keys, values = key_values(head, rows_v, left_v, right_v, rows_a, left_a, right_a)
        queries = jnp.concatenate([rows_v[head, :, :size], rows_a[head, :, :size]], 0)
        grad_out = jnp.concatenate([g[:, head * size : (head + 1) * size] for g in grads_out], 0)
        prob = soft(queries, keys, both_bias, factor)
        grad_prob = lax.dot_general(grad_out, values, NT, preferred_element_type=F32)
        center = jnp.sum(prob * grad_prob, -1, keepdims=True)
        dscore = (prob * (grad_prob - center) * factor).astype(BF16)
        dquery = jnp.dot(dscore, keys, preferred_element_type=F32)
        dkey = lax.dot_general(dscore, queries, TN, preferred_element_type=F32)
        dvalue = lax.dot_general(prob.astype(BF16), grad_out, TN, preferred_element_type=F32)
        for part, own in enumerate((own_v, own_a)):
            base = 3 * tokens * part
            middle = slice(base + tokens, base + 2 * tokens)
            own[head, :, :size] = dquery[part * tokens : (part + 1) * tokens]
            own[head, :, size : 2 * size] = dkey[middle]
            own[head, :, 2 * size :] = dvalue[middle]
            for target, start in ((to_left, base), (to_right, base + 2 * tokens)):
                target[part, head, :, :size] = dkey[start : start + tokens].astype(BF16)
                target[part, head, :, size:] = dvalue[start : start + tokens].astype(BF16)


def attend_back(keys, bias, grad_v, grad_a, w_out_v, w_out_a):
    heads, size, width = w_out_v.shape
    tokens = keys[0].shape[1]
    group = 2 if heads % 2 == 0 else 1
    whole = pl.BlockSpec((tokens, width), lambda i: (0, 0))
    own = jax.ShapeDtypeStruct((heads, tokens, 3 * size), F32)
    sent = jax.ShapeDtypeStruct((2, heads, tokens, 2 * size), BF16)
    sent_block = pl.BlockSpec((2, group, tokens, 2 * size), lambda i: (0, i, 0, 0))
    flops = 4 * heads * tokens * size * (30 * tokens + width)
    return pl.pallas_call(
        backward_kernel,
        grid=(heads // group,),
        out_shape=(own, own, sent, sent),
        in_specs=[head_block(group, array) for array in keys]
        + [
            pl.BlockSpec(bias.shape, lambda i: (0, 0, 0)),
            whole,
            whole,
            head_block(group, w_out_v),
            head_block(group, w_out_a),
        ],
        out_specs=(head_block(group, own), head_block(group, own), sent_block, sent_block),
        compiler_params=pltpu.CompilerParams(vmem_limit_bytes=40 * 2**20),
        cost_estimate=pl.CostEstimate(
            flops=flops, bytes_accessed=2 * heads * size * width * 2, transcendentals=0
        ),
        name="attend_back",
    )(*keys, bias, grad_v, grad_a, w_out_v, w_out_a)


def project(normed, weight):
    return jnp.einsum("nd,dhe->hne", normed, weight, preferred_element_type=F32).astype(BF16)


def inverse_rms(current):
    return lax.rsqrt(jnp.mean(current * current, -1, keepdims=True) + EPSILON)


def norm_back(current, inv_rms, modulation, grad_normed):
    scaled = grad_normed * modulation
    return inv_rms * scaled - current * inv_rms**3 * jnp.mean(scaled * current, -1, keepdims=True)


def local(
    video_tokens,
    audio_tokens,
    qkv_video,
    out_video,
    qkv_audio,
    out_audio,
    gain_video,
    gain_audio,
    time_from,
    time_to,
    time_steps,
    windows,
    intersection,
):
    tokens = video_tokens.shape[1]
    size = out_video.shape[1]
    bias, mods = prepare(
        time_steps, windows, intersection, time_from, time_to, gain_video, gain_audio, tokens
    )

    def normalise(current, inv_rms, row):
        return (current * inv_rms * mods[row : row + 1]).astype(BF16)

    def widen(normed_v, normed_a):
        keys = []
        for normed, weight in ((normed_v, qkv_video), (normed_a, qkv_audio)):
            rows = project(normed, weight)
            sent = rows[:, :, size:]
            keys += [rows, shift(sent, "vid", 1), shift(sent, "vid", -1)]
        return keys

    def network(normed_v, normed_a):
        keys = widen(normed_v, normed_a)
        heads_v, field_v = attend(keys, bias, out_video, 0)
        sum_v = sum_groups(field_v)
        heads_a, field_a = attend(keys, bias, out_audio, 1)
        sum_a = sum_groups(field_a)
        return sum_v, sum_a, heads_v, heads_a, keys

    start_v = video_tokens[0].astype(F32)
    start_a = audio_tokens[0].astype(F32)
    inv_v, inv_a = inverse_rms(start_v), inverse_rms(start_a)
    stride = time_steps[0, 1].astype(F32)
    euler_step = -stride / TGRID
    now_v, now_a = start_v, start_a
    for step in range(STEPS):
        field_v, field_a, *_ = network(
            normalise(now_v, inv_v if step == 0 else inverse_rms(now_v), 2 * step),
            normalise(now_a, inv_a if step == 0 else inverse_rms(now_a), 2 * step + 1),
        )
        now_v = now_v + euler_step * field_v
        now_a = now_a + euler_step * field_a
    normed_v = normalise(start_v, inv_v, 2 * STEPS)
    normed_a = normalise(start_a, inv_a, 2 * STEPS + 1)
    field_v, field_a, heads_v, heads_a, keys = network(normed_v, normed_a)

    norm_parts = scatter_columns(jnp.stack([normed_v, normed_a]))
    head_parts = gather_tokens(jnp.stack([heads_v, heads_a]))

    span = -(STEPS * stride) / TGRID
    diff_v = start_v + span * field_v - now_v
    diff_a = start_a + span * field_a - now_a
    grad_v = (span * diff_v).astype(BF16)
    grad_a = (span * diff_a).astype(BF16)
    own_v, own_a, to_left, to_right = attend_back(keys, bias, grad_v, grad_a, out_video, out_audio)
    grad_parts = scatter_columns(jnp.stack([grad_v, grad_a]))
    returned = shift(to_left, "vid", -1).astype(F32) + shift(to_right, "vid", 1).astype(F32)
    results = []
    for part, (own, weight, start, inv, row, diff) in enumerate(
        (
            (own_v, qkv_video, start_v, inv_v, 2 * STEPS, diff_v),
            (own_a, qkv_audio, start_a, inv_a, 2 * STEPS + 1, diff_a),
        )
    ):
        dqkv = jnp.concatenate(
            [own[:, :, :size], own[:, :, size:] + returned[part]], -1
        ).astype(BF16)
        dqkv_parts = gather_tokens(dqkv)
        back = sum_groups(
            jnp.einsum("hne,dhe->nd", dqkv, weight, preferred_element_type=F32).astype(BF16)
        )
        d_tokens = (diff + norm_back(start, inv, mods[row : row + 1], back)).astype(BF16)
        w_qkv = reduce_late(
            jnp.einsum(
                "slnd,shne->ldhe", norm_parts[:, :, part], dqkv_parts, preferred_element_type=F32
            )
        )
        w_out = reduce_late(
            jnp.einsum(
                "shne,slnf->lhef",
                head_parts[:, part],
                grad_parts[:, :, part],
                preferred_element_type=F32,
            )
        )
        results.append((d_tokens[None], w_qkv, w_out))
    (d_video, wqkv_v, wout_v), (d_audio, wqkv_a, wout_a) = results
    return (d_video, d_audio, wqkv_v, wout_v, wqkv_a, wout_a)


def solution(mesh):
    return jax.shard_map(
        local,
        mesh=mesh,
        in_specs=(
            P("clip", "vid", None),
            P("clip", "vid", None),
            P(None, "aud", None),
            P("aud", None, None),
            P(None, "aud", None),
            P("aud", None, None),
            P(),
            P(),
            P(),
            P(),
            P("clip", None),
            P("clip", None),
            P("clip", None, None),
        ),
        out_specs=(
            P("clip", "vid", None),
            P("clip", "vid", None),
            P(("clip", "vid"), "aud", None),
            P("aud", None, ("clip", "vid")),
            P(("clip", "vid"), "aud", None),
            P("aud", None, ("clip", "vid")),
        ),
        check_vma=False,
    )
```

```python
import functools

import jax
import jax.numpy as jnp
from jax import lax
from jax.experimental import pallas as pl
from jax.experimental.pallas import tpu as pltpu
from jax.sharding import PartitionSpec as P

BLK = 32
TGRID = 64
STEPS = 2
EPSILON = 1e-06
MASKED = -1e30
F32 = jnp.float32
BF16 = jnp.bfloat16
NT = (((1,), (1,)), ((), ()))
TN = (((0,), (0,)), ((), ()))
VMEM = 48 * 2**20


def swap(block, axis, bit):
    count = lax.axis_size(axis)
    return lax.ppermute(block, axis, [(i, i ^ (1 << bit)) for i in range(count)])


def shift(block, axis, distance):
    count = lax.axis_size(axis)
    route = [(i, i + distance) for i in range(count) if 0 <= i + distance < count]
    return lax.ppermute(block, axis, route)


def bits_of(count):
    return count.bit_length() - 1


def after(block, *first):
    return lax.optimization_barrier((block, first))[0]


def gather_steps(near_first):
    clip = [("clip", 0)] if lax.axis_size("clip") > 1 else []
    vid = [("vid", bit) for bit in reversed(range(bits_of(lax.axis_size("vid"))))]
    return clip + vid if near_first else vid[:-1] + clip + vid[-1:]


def gather_list(block, steps):
    blocks = [block]
    for axis, bit in steps:
        blocks = blocks + [swap(part, axis, bit) for part in blocks]
    return blocks


def scatter_parts(parts, steps):
    left = gather_steps(True)
    parts = parts[None]
    stages = []
    for axis, bit in steps:
        place = 2 + left.index((axis, bit))
        left.remove((axis, bit))
        keep = lax.index_in_dim(parts, 0, place, keepdims=False)
        send = lax.index_in_dim(parts, 1, place, keepdims=False)
        parts = jnp.concatenate([keep, swap(send, axis, bit)], 0)
        stages.append(parts)
    return stages


def source_order(wanted, held):
    return [
        sum((i >> b & 1) << held.index(step) for b, step in enumerate(wanted))
        for i in range(1 << len(wanted))
    ]


def device_dims():
    steps = gather_steps(True)
    devices = lax.axis_size("clip") * lax.axis_size("vid")
    return (devices >> len(steps),) + (2,) * len(steps)


LATE_BIT = 1


def exchange_groups(partial):
    count = lax.axis_size("aud")
    return [partial] + [
        lax.ppermute(partial, "aud", [(i, i ^ step) for i in range(count)])
        for step in range(1, count)
    ]


def prepare_kernel(
    steps, place, windows, lists, time_from, time_to, gain_v, gain_a, bias, mods, *, tokens
):
    time_now, stride = steps[0], steps[1]
    levels = [(time_now, time_now), (time_now - stride, time_now - stride)]
    levels.append((time_now, time_now - STEPS * stride))
    for row, (start, end) in enumerate(levels):
        condition = time_from[pl.ds(start, 1), :] + time_to[pl.ds(end, 1), :]
        mods[2 * row : 2 * row + 1, :] = gain_v[...] * (1.0 + condition)
        mods[2 * row + 1 : 2 * row + 2, :] = gain_a[...] * (1.0 + condition)

    device = place[0]
    blocks = tokens // BLK
    all_blocks = place[1]
    shape = (tokens, 3 * tokens)
    row_pos = device * tokens + lax.broadcasted_iota(jnp.int32, shape, 0)
    column = lax.broadcasted_iota(jnp.int32, shape, 1)
    column_pos = (device - 1) * tokens + column
    inside = (column_pos >= 0) & (column_pos < all_blocks * BLK)
    distance = jnp.abs(row_pos - column_pos)
    row_blk = device * blocks + lax.broadcasted_iota(jnp.int32, shape, 0) // BLK
    column_blk = (device - 1) * blocks + column // BLK

    def fill(admitted, part, side):
        bias[part, :, side * 3 * tokens : (side + 1) * 3 * tokens] = jnp.where(
            admitted, 0.0, MASKED
        ).astype(F32)

    fill(inside & (distance < windows[0]), 0, 0)
    fill(inside & (distance < windows[1]), 1, 1)
    low = jnp.zeros(shape, jnp.int32)
    high = jnp.zeros(shape, jnp.int32)
    for block in range(blocks):
        here = row_blk == device * blocks + block
        low = jnp.where(here, lists[device * blocks + block, 0], low)
        high = jnp.where(here, lists[device * blocks + block, 1], high)
    fill(inside & (column_blk >= low) & (column_blk < high), 0, 1)
    low = jnp.zeros(shape, jnp.int32)
    high = jnp.zeros(shape, jnp.int32)
    for block in range(3 * blocks):
        index = (device - 1) * blocks + block
        safe = jnp.clip(index, 0, all_blocks - 1)
        here = column_blk == index
        low = jnp.where(here, lists[safe, 0], low)
        high = jnp.where(here, lists[safe, 1], high)
    fill(inside & (row_blk >= low) & (row_blk < high), 1, 0)


def prepare(time_steps, windows, intersection, time_from, time_to, gain_video, gain_audio, tokens):
    place = jnp.stack([lax.axis_index("vid"), lax.axis_size("vid") * tokens // BLK])
    smem = pl.BlockSpec(memory_space=pltpu.SMEM)
    vmem = pl.BlockSpec(memory_space=pltpu.VMEM)
    width = gain_video.shape[0]
    return pl.pallas_call(
        functools.partial(prepare_kernel, tokens=tokens),
        out_shape=(
            jax.ShapeDtypeStruct((2, tokens, 6 * tokens), F32),
            jax.ShapeDtypeStruct((6, width), F32),
        ),
        in_specs=[smem] * 4 + [vmem] * 4,
        out_specs=(vmem, vmem),
        name="prepare",
    )(
        time_steps[0],
        place.astype(jnp.int32),
        windows[0],
        intersection[0],
        time_from,
        time_to,
        gain_video[None],
        gain_audio[None],
    )


def soft(queries, keys, bias, factor):
    scores = lax.dot_general(queries, keys, NT, preferred_element_type=F32) * factor + bias
    shifted = jnp.exp(scores - jnp.max(scores, -1, keepdims=True))
    return shifted * (1.0 / jnp.sum(shifted, -1, keepdims=True))


def key_values(head, rows_v, left_v, right_v, rows_a, left_a, right_a):
    size = left_v.shape[-1] // 2
    keys, values = [], []
    for left, rows, right in ((left_v, rows_v, right_v), (left_a, rows_a, right_a)):
        keys += [left[head, :, :size], rows[head, :, size : 2 * size], right[head, :, :size]]
        values += [left[head, :, size:], rows[head, :, 2 * size :], right[head, :, size:]]
    return jnp.concatenate(keys, 0), jnp.concatenate(values, 0)


def forward_kernel(*refs, parts, mixed, waits, turned):
    rows_v, left_v, right_v, rows_a, left_a, right_a, bias = refs[:7]
    w_outs = refs[7 : 7 + len(parts)]
    at = 7 + len(parts)
    coef, other = refs[at : at + 2] if mixed else (None, None)
    heads_out, field, total = refs[at + 2 * mixed + waits :]
    step = pl.program_id(0)
    group, tokens, size = rows_v.shape[0], rows_v.shape[1], left_v.shape[-1] // 2
    outs = [[] for _ in parts]
    for head in range(group):
        keys, values = key_values(head, rows_v, left_v, right_v, rows_a, left_a, right_a)
        queries = jnp.concatenate([(rows_v, rows_a)[part][head, :, :size] for part in parts], 0)
        prob = soft(queries, keys, bias[...].reshape(-1, bias.shape[-1]), size**-0.5)
        out = jnp.dot(prob.astype(BF16), values, preferred_element_type=F32).astype(BF16)
        for index in range(len(parts)):
            outs[index].append(out[index * tokens : (index + 1) * tokens])
            heads_out[index, head] = outs[index][-1].T if turned else outs[index][-1]
    for index, w_out in enumerate(w_outs):
        term = jnp.dot(
            jnp.concatenate(outs[index], 1),
            w_out[...].reshape(group * size, w_out.shape[-1]),
            preferred_element_type=F32,
        )
        total[index] = jnp.where(step == 0, 0.0, total[index]) + term

    @pl.when(step == pl.num_programs(0) - 1)
    def _():
        result = total[...]
        if mixed:
            result = coef[0] * other[...] + coef[1] * result
        field[...] = result.astype(field.dtype)


def head_block(group, array, first=0):
    return pl.BlockSpec((group,) + array.shape[1:], lambda i: (i + first // group, 0, 0))


def attend(keys, bias, w_outs, parts, dtype=BF16, mix=(), waits=(), turned=False):
    heads, size, width = w_outs[0].shape
    tokens = keys[0].shape[1]
    group = 2 if heads % 2 == 0 else 1
    number = len(parts)
    out_dims = (size, tokens) if turned else (tokens, size)
    flops = 2 * number * heads * tokens * size * (12 * tokens + width)
    whole = pl.BlockSpec((number, tokens, width), lambda i: (0, 0, 0))
    one = pl.BlockSpec((1, tokens, width), lambda i: (parts[0], 0, 0))
    return pl.pallas_call(
        functools.partial(forward_kernel, parts=parts, mixed=bool(mix), waits=len(waits), turned=turned),
        grid=(heads // group,),
        out_shape=(
            jax.ShapeDtypeStruct((number, heads) + out_dims, BF16),
            jax.ShapeDtypeStruct((number, tokens, width), dtype),
        ),
        in_specs=[head_block(group, array) for array in keys]
        + [pl.BlockSpec((number,) + bias.shape[1:], lambda i: (parts[0], 0, 0))]
        + [head_block(group, w_out) for w_out in w_outs]
        + ([pl.BlockSpec(memory_space=pltpu.SMEM), one] if mix else [])
        + [pl.BlockSpec(memory_space=pl.ANY)] * len(waits),
        out_specs=(
            pl.BlockSpec((number, group) + out_dims, lambda i: (0, i, 0, 0)),
            whole,
        ),
        scratch_shapes=[pltpu.VMEM((number, tokens, width), F32)],
        compiler_params=pltpu.CompilerParams(vmem_limit_bytes=VMEM),
        cost_estimate=pl.CostEstimate(
            flops=flops, bytes_accessed=number * heads * size * width * 2, transcendentals=0
        ),
        name="attend",
    )(*keys, bias, *w_outs, *mix, *waits)


def backward_kernel(
    rows_v,
    left_v,
    right_v,
    rows_a,
    left_a,
    right_a,
    bias,
    grad_v,
    grad_a,
    w_out_v,
    w_out_a,
    *rest,
):
    own_v, own_a, to_left, to_right = rest[-4:]
    group, tokens, triple = rows_v.shape
    size = triple // 3
    factor = size**-0.5
    both_bias = bias[...].reshape(2 * tokens, 6 * tokens)
    width = w_out_v.shape[-1]
    grads_out = [
        lax.dot_general(
            grad[...], w_out[...].reshape(group * size, width), NT, preferred_element_type=F32
        ).astype(BF16)
        for grad, w_out in ((grad_v, w_out_v), (grad_a, w_out_a))
    ]
    for head in range(group):
        keys, values = key_values(head, rows_v, left_v, right_v, rows_a, left_a, right_a)
        queries = jnp.concatenate([rows_v[head, :, :size], rows_a[head, :, :size]], 0)
        grad_out = jnp.concatenate([g[:, head * size : (head + 1) * size] for g in grads_out], 0)
        prob = soft(queries, keys, both_bias, factor)
        grad_prob = lax.dot_general(grad_out, values, NT, preferred_element_type=F32)
        center = jnp.sum(prob * grad_prob, -1, keepdims=True)
        dscore = (prob * (grad_prob - center) * factor).astype(BF16)
        dquery = jnp.dot(dscore, keys, preferred_element_type=F32)
        dkey = lax.dot_general(dscore, queries, TN, preferred_element_type=F32)
        dvalue = lax.dot_general(prob.astype(BF16), grad_out, TN, preferred_element_type=F32)
        for part, own in enumerate((own_v, own_a)):
            base = 3 * tokens * part
            middle = slice(base + tokens, base + 2 * tokens)
            own[head, :, :size] = dquery[part * tokens : (part + 1) * tokens]
            own[head, :, size : 2 * size] = dkey[middle]
            own[head, :, 2 * size :] = dvalue[middle]
            for target, start in ((to_left, base), (to_right, base + 2 * tokens)):
                target[part, head, :, :size] = dkey[start : start + tokens].astype(BF16)
                target[part, head, :, size:] = dvalue[start : start + tokens].astype(BF16)


def attend_back(keys, bias, grad_v, grad_a, w_out_v, w_out_a, first, heads, waits):
    size, width = w_out_v.shape[1:]
    tokens = keys[0].shape[1]
    group = 2 if heads % 2 == 0 and first % 2 == 0 else 1
    own = jax.ShapeDtypeStruct((heads, tokens, 3 * size), F32)
    sent = jax.ShapeDtypeStruct((2, heads, tokens, 2 * size), BF16)
    sent_block = pl.BlockSpec((2, group, tokens, 2 * size), lambda i: (0, i, 0, 0))
    flops = 4 * heads * tokens * size * (30 * tokens + width)
    return pl.pallas_call(
        backward_kernel,
        grid=(heads // group,),
        out_shape=(own, own, sent, sent),
        in_specs=[head_block(group, array, first) for array in keys]
        + [
            pl.BlockSpec(bias.shape, lambda i: (0, 0, 0)),
            pl.BlockSpec(grad_v.shape, lambda i: (0, 0)),
            pl.BlockSpec(grad_a.shape, lambda i: (0, 0)),
            head_block(group, w_out_v, first),
            head_block(group, w_out_a, first),
        ]
        + [pl.BlockSpec(memory_space=pl.ANY)] * len(waits),
        out_specs=(head_block(group, own), head_block(group, own), sent_block, sent_block),
        compiler_params=pltpu.CompilerParams(vmem_limit_bytes=VMEM),
        cost_estimate=pl.CostEstimate(
            flops=flops, bytes_accessed=2 * heads * size * width * 2, transcendentals=0
        ),
        name="attend_back",
    )(*keys, bias, grad_v, grad_a, w_out_v, w_out_a, *waits)


def assemble_kernel(own_v, own_a, first, second, *rest):
    size = own_v.shape[-1] // 3
    out = rest[-1]
    for part, own in enumerate((own_v, own_a)):
        out[part, :, :, :size] = own[:, :, :size].astype(BF16)
        out[part, :, :, size:] = (
            own[:, :, size:] + first[part].astype(F32) + second[part].astype(F32)
        ).astype(BF16)


def assemble(own_v, own_a, first, second, waits):
    vmem = pl.BlockSpec(memory_space=pltpu.VMEM)
    return pl.pallas_call(
        assemble_kernel,
        out_shape=jax.ShapeDtypeStruct((2,) + own_v.shape, BF16),
        in_specs=[vmem] * 4 + [pl.BlockSpec(memory_space=pl.ANY)] * len(waits),
        out_specs=vmem,
        compiler_params=pltpu.CompilerParams(vmem_limit_bytes=VMEM),
        name="assemble",
    )(own_v, own_a, first, second, *waits)


def advance_kernel(coef, mods, start, *refs, terms):
    now, normed = refs[-2:]
    value = start[...].astype(F32) + coef[0] * sum(ref[...].astype(F32) for ref in refs[:terms])
    now[...] = value
    inv_rms = lax.rsqrt(jnp.mean(value * value, -1, keepdims=True) + EPSILON)
    normed[...] = (value * inv_rms * mods[...]).astype(BF16)


def advance(coef, mods, start, sums, waits):
    vmem = pl.BlockSpec(memory_space=pltpu.VMEM)
    return pl.pallas_call(
        functools.partial(advance_kernel, terms=len(sums)),
        out_shape=(
            jax.ShapeDtypeStruct(start.shape, F32),
            jax.ShapeDtypeStruct(start.shape, BF16),
        ),
        in_specs=[pl.BlockSpec(memory_space=pltpu.SMEM)]
        + [vmem] * (2 + len(sums))
        + [pl.BlockSpec(memory_space=pl.ANY)] * len(waits),
        out_specs=(vmem, vmem),
        compiler_params=pltpu.CompilerParams(vmem_limit_bytes=VMEM),
        name="advance",
    )(coef, mods, start, *sums, *waits)


def turn_kernel(place, first, second, out):
    devices, _, rows, _ = out.shape
    for part, ref in enumerate((first, second)):
        turned = ref[...].T
        for device in range(devices):
            out[device ^ place[0], part] = turned[device * rows : (device + 1) * rows]


def turn(place, first, second):
    vmem = pl.BlockSpec(memory_space=pltpu.VMEM)
    devices = lax.axis_size("clip") * lax.axis_size("vid")
    tokens, width = first.shape
    return pl.pallas_call(
        turn_kernel,
        out_shape=jax.ShapeDtypeStruct((devices, 2, width // devices, tokens), BF16),
        in_specs=[pl.BlockSpec(memory_space=pltpu.SMEM), vmem, vmem],
        out_specs=vmem,
        compiler_params=pltpu.CompilerParams(vmem_limit_bytes=VMEM),
        name="turn",
    )(place, first, second)


def differ_kernel(place, coef, start, now, *refs, terms):
    diff, grads, columns = refs[-3:]
    devices, _, wide = columns.shape
    value = start[...].astype(F32) - now[...]
    value = value + sum(ref[...].astype(F32) for ref in refs[:terms])
    diff[...] = value
    grad = (coef[0] * value).astype(BF16)
    grads[...] = grad
    for device in range(devices):
        columns[device ^ place[0]] = grad[:, device * wide : (device + 1) * wide]


def differ(place, coef, start, now, sums, waits):
    vmem = pl.BlockSpec(memory_space=pltpu.VMEM)
    smem = pl.BlockSpec(memory_space=pltpu.SMEM)
    devices = lax.axis_size("clip") * lax.axis_size("vid")
    tokens, width = start.shape
    return pl.pallas_call(
        functools.partial(differ_kernel, terms=len(sums)),
        out_shape=(
            jax.ShapeDtypeStruct((tokens, width), F32),
            jax.ShapeDtypeStruct((tokens, width), BF16),
            jax.ShapeDtypeStruct((devices, tokens, width // devices), BF16),
        ),
        in_specs=[smem, smem]
        + [vmem] * (2 + len(sums))
        + [pl.BlockSpec(memory_space=pl.ANY)] * len(waits),
        out_specs=(vmem,) * 3,
        compiler_params=pltpu.CompilerParams(vmem_limit_bytes=VMEM),
        name="differ",
    )(place, coef, start, now, *sums, *waits)


def weight_kernel(turned, *refs, parts, order):
    keep, send = refs[-2:]
    rows = keep.shape[1]
    blocks = []
    for ref in refs[:parts]:
        blocks += [ref[source, 0, 0] for source in range(ref.shape[0])]
    left = [
        jnp.concatenate([turned[source, late, 0] for source in order], 1) for late in range(2)
    ]
    result = jnp.dot(
        jnp.concatenate(left, 0), jnp.concatenate(blocks, 0), preferred_element_type=F32
    )
    keep[0] = result[:rows]
    send[0] = result[rows:].astype(BF16)


def weight_terms(turned, part, parts, order, waits):
    heads, tokens, width = parts[0].shape[2:]
    sources, late, _, rows, _ = turned.shape
    block = pl.BlockSpec((1, rows, width), lambda i: (i, 0, 0))
    return pl.pallas_call(
        functools.partial(weight_kernel, parts=len(parts), order=order),
        grid=(heads,),
        out_shape=(
            jax.ShapeDtypeStruct((heads, rows, width), F32),
            jax.ShapeDtypeStruct((heads, rows, width), BF16),
        ),
        in_specs=[pl.BlockSpec((sources, late, 1, rows, tokens), lambda i: (0, 0, part, 0, 0))]
        + [
            pl.BlockSpec((piece.shape[0], 1, 1, tokens, width), lambda i: (0, part, i, 0, 0))
            for piece in parts
        ]
        + [pl.BlockSpec(memory_space=pl.ANY)] * len(waits),
        out_specs=(block, block),
        compiler_params=pltpu.CompilerParams(vmem_limit_bytes=VMEM),
        name="weight_terms",
    )(turned, *parts, *waits)


def out_kernel(grads, *refs):
    keep, send = refs[-2:]
    wide = keep.shape[-1]
    heads_out = jnp.concatenate([ref[0, 0] for ref in refs[:-2]], 1)
    right = jnp.concatenate(
        [
            jnp.concatenate([grads[source, late] for late in range(2)], 1)
            for source in range(grads.shape[0])
        ],
        0,
    )
    result = jnp.dot(heads_out, right, preferred_element_type=F32)
    keep[0] = result[:, :wide]
    send[0] = result[:, wide:].astype(BF16)


def out_terms(grads, pieces, part):
    _, heads, size, tokens = pieces[0].shape
    wide = grads.shape[-1]
    block = pl.BlockSpec((1, size, wide), lambda i: (i, 0, 0))
    return pl.pallas_call(
        out_kernel,
        grid=(heads,),
        out_shape=(
            jax.ShapeDtypeStruct((heads, size, wide), F32),
            jax.ShapeDtypeStruct((heads, size, wide), BF16),
        ),
        in_specs=[pl.BlockSpec(grads.shape, lambda i: (0, 0, 0, 0))]
        + [pl.BlockSpec((1, 1, size, tokens), lambda i: (part, i, 0, 0))] * len(pieces),
        out_specs=(block, block),
        compiler_params=pltpu.CompilerParams(vmem_limit_bytes=VMEM),
        name="out_terms",
    )(grads, *pieces)


def project(normed, weight):
    return jnp.einsum("nd,dhe->hne", normed, weight, preferred_element_type=F32).astype(BF16)


def inverse_rms(current):
    return lax.rsqrt(jnp.mean(current * current, -1, keepdims=True) + EPSILON)


def norm_back(current, inv_rms, modulation, grad_normed):
    scaled = grad_normed * modulation
    return inv_rms * scaled - current * inv_rms**3 * jnp.mean(scaled * current, -1, keepdims=True)


def local(
    video_tokens,
    audio_tokens,
    qkv_video,
    out_video,
    qkv_audio,
    out_audio,
    gain_video,
    gain_audio,
    time_from,
    time_to,
    time_steps,
    windows,
    intersection,
):
    tokens = video_tokens.shape[1]
    size = out_video.shape[1]
    bias, mods = prepare(
        time_steps, windows, intersection, time_from, time_to, gain_video, gain_audio, tokens
    )

    def normalise(current, inv_rms, row):
        return (current * inv_rms * mods[row : row + 1]).astype(BF16)

    def widen(normed, weight):
        rows = project(normed, weight)
        sent = rows[:, :, size:]
        return [rows, shift(sent, "vid", 1), shift(sent, "vid", -1)]

    start_v = video_tokens[0].astype(F32)
    start_a = audio_tokens[0].astype(F32)
    inv_v, inv_a = inverse_rms(start_v), inverse_rms(start_a)
    stride = time_steps[0, 1].astype(F32)
    euler_step = -stride / TGRID
    span = -(STEPS * stride) / TGRID
    near, far = gather_steps(True), gather_steps(False)
    heads = out_video.shape[0]

    normed_v = normalise(start_v, inv_v, 2 * STEPS)
    normed_a = normalise(start_a, inv_a, 2 * STEPS + 1)
    place = lax.axis_index(("clip", "vid"))[None].astype(jnp.int32)
    dims = device_dims()
    now_v, now_a = video_tokens[0], audio_tokens[0]
    for step in range(STEPS):
        first, last = step == 0, step == STEPS - 1
        if first:
            keys = widen(normalise(start_v, inv_v, 0), qkv_video)
            keys += widen(normalise(start_a, inv_a, 1), qkv_audio)
        else:
            keys = widen(next_v, qkv_video)
            now_a, next_a = advance(
                euler_step[None], mods[row + 1 : row + 2], now_a, sums_a, (keys[0],)
            )
            keys += widen(next_a, qkv_audio)
        if first:
            student = widen(after(normed_v, keys[0], keys[3]), qkv_video)
            waits = ((student[0],), tuple(student[1:3]))
        else:
            waits = ((), ())
        if last:
            turned = turn(place, normed_v, after(normed_a, keys[0]))
            norm_stages = scatter_parts(turned.reshape(dims + turned.shape[1:]), far)
            norm_parts = norm_stages[-1]
            waits = ((), (norm_stages[0],))
            student_heads, student_field = attend(
                student,
                bias,
                (out_video, out_audio),
                (0, 1),
                F32,
                waits=(keys[3],),
                turned=True,
            )
            pieces = gather_list(student_heads, far)
        mix = (jnp.stack([span, -euler_step]), student_field) if last else ()
        _, field_v = attend(keys, bias, (out_video,), (0,), mix=mix, waits=waits[0])
        sums_v = exchange_groups(field_v[0])
        _, field_a = attend(keys, bias, (out_audio,), (1,), mix=mix, waits=(field_v,) + waits[1])
        sums_a = exchange_groups(field_a[0])
        if first:
            student += widen(after(normed_a, field_a), qkv_audio)
        if not last:
            row = 2 * step + 2
            now_v, next_v = advance(
                euler_step[None], mods[row : row + 1], now_v, sums_v, (student[3],)
            )
    diff_v, grad_v, columns = differ(
        place, span[None], video_tokens[0], now_v, sums_v, (*pieces[1:2], norm_stages[1])
    )
    stages_v = scatter_parts(columns.reshape(dims + columns.shape[1:]), far)
    diff_a, grad_a, columns = differ(
        place, span[None], audio_tokens[0], now_a, sums_a, (*pieces[2:4], stages_v[0])
    )
    stages_a = scatter_parts(columns.reshape(dims + columns.shape[1:]), far)

    halves = 2 if heads % 4 == 0 else 1
    count = heads // halves
    backs = []
    for half in range(halves):
        backs.append(
            attend_back(
                student,
                bias,
                grad_v,
                grad_a,
                out_video,
                out_audio,
                half * count,
                count,
                (backs[-1][2], *pieces[4:], norm_parts, stages_v[1], stages_a[0]) if half > 0 else (),
            )
        )
    out_v = out_terms(stages_v[-1], pieces, 0)
    out_a = out_terms(stages_a[-1], pieces, 1)
    chunks = []
    for half, (own_v, own_a, to_left, to_right) in enumerate(backs):
        waits = (backs[-1][2],) if half == 0 else (out_v[1],)
        chunks.append(
            assemble(own_v, own_a, shift(to_left, "vid", -1), shift(to_right, "vid", 1), waits)
        )

    out_came_v = swap(out_v[1], "clip", LATE_BIT)
    out_came_a = swap(out_a[1], "clip", LATE_BIT)

    terms = []
    line = {}

    def in_line(block, *key):
        line[key] = swap(after(block, line[key]) if key in line else block, *key)
        return line[key]

    backs = []
    for part in range(2):
        backs.append(jnp.concatenate([chunk[part] for chunk in chunks], 0))
    held = [((chunks[-1], stages_a[1]), (out_a[1],))]
    for index, (chunk, steps) in enumerate(zip(chunks, (near, far))):
        blocks = [chunk]
        for level, step in enumerate(steps[:-1]):
            if level > 0:
                blocks[1] = after(blocks[1], *held[-1][0])
            blocks = blocks + [in_line(block, *step) for block in blocks]
        blocks[-1] = after(blocks[-1], *held[-1][1])
        parts = [jnp.stack(blocks)]
        for axis, bit in steps[-1:]:
            parts.append(swap(parts[0], axis, bit))
        both = []
        for part in range(2):
            keep, send = weight_terms(
                norm_parts,
                part,
                parts,
                source_order(steps, far),
                (both[0][1],) if part else (out_came_a,) * index,
            )
            both.append((keep, send, swap(send, "clip", LATE_BIT)))
        terms.append(both)
        if index == 0:
            backs = [
                jnp.einsum(
                    "hne,dhe->nd", after(dqkv, both[1][1]), weight, preferred_element_type=F32
                ).astype(BF16)
                for dqkv, weight in zip(backs, (qkv_video, qkv_audio))
            ]
        held.append(((both[1][1], out_came_v), (both[0][2], both[1][2], *backs)))

    final = terms[-1][1][1]
    w_out = [
        after(keep, final) + came.astype(F32)
        for keep, came in ((out_v[0], out_came_v), (out_a[0], out_came_a))
    ]
    results = []
    for part, (start, inv, row, diff) in enumerate(
        (
            (start_v, inv_v, 2 * STEPS, diff_v),
            (start_a, inv_a, 2 * STEPS + 1, diff_a),
        )
    ):
        back = sum(
            after(partial, final).astype(F32) for partial in exchange_groups(backs[part])
        )
        diff = after(diff, final)
        d_tokens = (diff + norm_back(start, inv, mods[row : row + 1], back)).astype(BF16)
        grad_qkv = jnp.concatenate(
            [after(both[part][0], final) + both[part][2].astype(F32) for both in terms], 0
        ).transpose(1, 0, 2)
        results.append((d_tokens[None], grad_qkv, w_out[part]))
    (d_video, wqkv_v, wout_v), (d_audio, wqkv_a, wout_a) = results
    return (d_video, d_audio, wqkv_v, wout_v, wqkv_a, wout_a)


def solution(mesh):
    return jax.shard_map(
        local,
        mesh=mesh,
        in_specs=(
            P("clip", "vid", None),
            P("clip", "vid", None),
            P(None, "aud", None),
            P("aud", None, None),
            P(None, "aud", None),
            P("aud", None, None),
            P(),
            P(),
            P(),
            P(),
            P("clip", None),
            P("clip", None),
            P("clip", None, None),
        ),
        out_specs=(
            P("clip", "vid", None),
            P("clip", "vid", None),
            P(("clip", "vid"), "aud", None),
            P("aud", None, ("clip", "vid")),
            P(("clip", "vid"), "aud", None),
            P("aud", None, ("clip", "vid")),
        ),
        check_vma=False,
    )
```

```python
import functools

import jax
import jax.numpy as jnp
from jax import lax
from jax.experimental import pallas as pl
from jax.experimental.pallas import tpu as pltpu
from jax.sharding import PartitionSpec as P

BLK = 32
TGRID = 64
STEPS = 2
EPSILON = 1e-06
MASKED = -1e30
F32 = jnp.float32
BF16 = jnp.bfloat16
NT = (((1,), (1,)), ((), ()))
TN = (((0,), (0,)), ((), ()))
VMEM = 48 * 2**20


def swap(block, axis, bit):
    count = lax.axis_size(axis)
    return lax.ppermute(block, axis, [(i, i ^ (1 << bit)) for i in range(count)])


def shift(block, axis, distance):
    count = lax.axis_size(axis)
    route = [(i, i + distance) for i in range(count) if 0 <= i + distance < count]
    return lax.ppermute(block, axis, route)


def bits_of(count):
    return count.bit_length() - 1


def after(block, *first):
    return lax.optimization_barrier((block, first))[0]


def gather_steps(near_first):
    clip = [("clip", 0)] if lax.axis_size("clip") > 1 else []
    vid = [("vid", bit) for bit in reversed(range(bits_of(lax.axis_size("vid"))))]
    return clip + vid if near_first else vid[:-1] + clip + vid[-1:]


def gather_list(block, steps):
    blocks = [block]
    for axis, bit in steps:
        blocks = blocks + [swap(part, axis, bit) for part in blocks]
    return blocks


def scatter_parts(parts, steps):
    left = gather_steps(True)
    parts = parts[None]
    stages = []
    for axis, bit in steps:
        place = 2 + left.index((axis, bit))
        left.remove((axis, bit))
        keep = lax.index_in_dim(parts, 0, place, keepdims=False)
        send = lax.index_in_dim(parts, 1, place, keepdims=False)
        parts = jnp.concatenate([keep, swap(send, axis, bit)], 0)
        stages.append(parts)
    return stages


def source_order(wanted, held):
    return [
        sum((i >> b & 1) << held.index(step) for b, step in enumerate(wanted))
        for i in range(1 << len(wanted))
    ]


def device_dims():
    steps = gather_steps(True)
    devices = lax.axis_size("clip") * lax.axis_size("vid")
    return (devices >> len(steps),) + (2,) * len(steps)


LATE_BIT = 1


def exchange_groups(partial):
    count = lax.axis_size("aud")
    return [partial] + [
        lax.ppermute(partial, "aud", [(i, i ^ step) for i in range(count)])
        for step in range(1, count)
    ]


def prepare_kernel(
    steps, place, windows, lists, time_from, time_to, gain_v, gain_a, bias, mods, *, tokens
):
    time_now, stride = steps[0], steps[1]
    levels = [(time_now, time_now), (time_now - stride, time_now - stride)]
    levels.append((time_now, time_now - STEPS * stride))
    for row, (start, end) in enumerate(levels):
        condition = time_from[pl.ds(start, 1), :] + time_to[pl.ds(end, 1), :]
        mods[2 * row : 2 * row + 1, :] = gain_v[...] * (1.0 + condition)
        mods[2 * row + 1 : 2 * row + 2, :] = gain_a[...] * (1.0 + condition)

    device = place[0]
    blocks = tokens // BLK
    all_blocks = place[1]
    shape = (tokens, 3 * tokens)
    row_pos = device * tokens + lax.broadcasted_iota(jnp.int32, shape, 0)
    column = lax.broadcasted_iota(jnp.int32, shape, 1)
    column_pos = (device - 1) * tokens + column
    inside = (column_pos >= 0) & (column_pos < all_blocks * BLK)
    distance = jnp.abs(row_pos - column_pos)
    row_blk = device * blocks + lax.broadcasted_iota(jnp.int32, shape, 0) // BLK
    column_blk = (device - 1) * blocks + column // BLK

    def fill(admitted, part, side):
        bias[part, :, side * 3 * tokens : (side + 1) * 3 * tokens] = jnp.where(
            admitted, 0.0, MASKED
        ).astype(F32)

    fill(inside & (distance < windows[0]), 0, 0)
    fill(inside & (distance < windows[1]), 1, 1)
    low = jnp.zeros(shape, jnp.int32)
    high = jnp.zeros(shape, jnp.int32)
    for block in range(blocks):
        here = row_blk == device * blocks + block
        low = jnp.where(here, lists[device * blocks + block, 0], low)
        high = jnp.where(here, lists[device * blocks + block, 1], high)
    fill(inside & (column_blk >= low) & (column_blk < high), 0, 1)
    low = jnp.zeros(shape, jnp.int32)
    high = jnp.zeros(shape, jnp.int32)
    for block in range(3 * blocks):
        index = (device - 1) * blocks + block
        safe = jnp.clip(index, 0, all_blocks - 1)
        here = column_blk == index
        low = jnp.where(here, lists[safe, 0], low)
        high = jnp.where(here, lists[safe, 1], high)
    fill(inside & (row_blk >= low) & (row_blk < high), 1, 0)


def prepare(time_steps, windows, intersection, time_from, time_to, gain_video, gain_audio, tokens):
    place = jnp.stack([lax.axis_index("vid"), lax.axis_size("vid") * tokens // BLK])
    smem = pl.BlockSpec(memory_space=pltpu.SMEM)
    vmem = pl.BlockSpec(memory_space=pltpu.VMEM)
    width = gain_video.shape[0]
    return pl.pallas_call(
        functools.partial(prepare_kernel, tokens=tokens),
        out_shape=(
            jax.ShapeDtypeStruct((2, tokens, 6 * tokens), F32),
            jax.ShapeDtypeStruct((6, width), F32),
        ),
        in_specs=[smem] * 4 + [vmem] * 4,
        out_specs=(vmem, vmem),
        name="prepare",
    )(
        time_steps[0],
        place.astype(jnp.int32),
        windows[0],
        intersection[0],
        time_from,
        time_to,
        gain_video[None],
        gain_audio[None],
    )


def soft(queries, keys, bias, factor):
    scores = lax.dot_general(queries, keys, NT, preferred_element_type=F32) * factor + bias
    shifted = jnp.exp(scores - jnp.max(scores, -1, keepdims=True))
    return shifted * (1.0 / jnp.sum(shifted, -1, keepdims=True))


def key_values(head, rows_v, left_v, right_v, rows_a, left_a, right_a):
    size = left_v.shape[-1] // 2
    keys, values = [], []
    for left, rows, right in ((left_v, rows_v, right_v), (left_a, rows_a, right_a)):
        keys += [left[head, :, :size], rows[head, :, size : 2 * size], right[head, :, :size]]
        values += [left[head, :, size:], rows[head, :, 2 * size :], right[head, :, size:]]
    return jnp.concatenate(keys, 0), jnp.concatenate(values, 0)


def forward_kernel(*refs, parts, mixed, waits, turned):
    rows_v, left_v, right_v, rows_a, left_a, right_a, bias = refs[:7]
    w_outs = refs[7 : 7 + len(parts)]
    at = 7 + len(parts)
    coef, other = refs[at : at + 2] if mixed else (None, None)
    heads_out, field, total = refs[at + 2 * mixed + waits :]
    step = pl.program_id(0)
    group, tokens, size = rows_v.shape[0], rows_v.shape[1], left_v.shape[-1] // 2
    outs = [[] for _ in parts]
    for head in range(group):
        keys, values = key_values(head, rows_v, left_v, right_v, rows_a, left_a, right_a)
        queries = jnp.concatenate([(rows_v, rows_a)[part][head, :, :size] for part in parts], 0)
        prob = soft(queries, keys, bias[...].reshape(-1, bias.shape[-1]), size**-0.5)
        out = jnp.dot(prob.astype(BF16), values, preferred_element_type=F32).astype(BF16)
        for index in range(len(parts)):
            outs[index].append(out[index * tokens : (index + 1) * tokens])
            heads_out[index, head] = outs[index][-1].T if turned else outs[index][-1]
    for index, w_out in enumerate(w_outs):
        term = jnp.dot(
            jnp.concatenate(outs[index], 1),
            w_out[...].reshape(group * size, w_out.shape[-1]),
            preferred_element_type=F32,
        )
        total[index] = jnp.where(step == 0, 0.0, total[index]) + term

    @pl.when(step == pl.num_programs(0) - 1)
    def _():
        result = total[...]
        if mixed:
            result = coef[0] * other[...] + coef[1] * result
        field[...] = result.astype(field.dtype)


def head_block(group, array, first=0):
    return pl.BlockSpec((group,) + array.shape[1:], lambda i: (i + first // group, 0, 0))


def attend(keys, bias, w_outs, parts, dtype=BF16, mix=(), waits=(), turned=False):
    heads, size, width = w_outs[0].shape
    tokens = keys[0].shape[1]
    group = 2 if heads % 2 == 0 else 1
    number = len(parts)
    out_dims = (size, tokens) if turned else (tokens, size)
    flops = 2 * number * heads * tokens * size * (12 * tokens + width)
    whole = pl.BlockSpec((number, tokens, width), lambda i: (0, 0, 0))
    one = pl.BlockSpec((1, tokens, width), lambda i: (parts[0], 0, 0))
    return pl.pallas_call(
        functools.partial(forward_kernel, parts=parts, mixed=bool(mix), waits=len(waits), turned=turned),
        grid=(heads // group,),
        out_shape=(
            jax.ShapeDtypeStruct((number, heads) + out_dims, BF16),
            jax.ShapeDtypeStruct((number, tokens, width), dtype),
        ),
        in_specs=[head_block(group, array) for array in keys]
        + [pl.BlockSpec((number,) + bias.shape[1:], lambda i: (parts[0], 0, 0))]
        + [head_block(group, w_out) for w_out in w_outs]
        + ([pl.BlockSpec(memory_space=pltpu.SMEM), one] if mix else [])
        + [pl.BlockSpec(memory_space=pl.ANY)] * len(waits),
        out_specs=(
            pl.BlockSpec((number, group) + out_dims, lambda i: (0, i, 0, 0)),
            whole,
        ),
        scratch_shapes=[pltpu.VMEM((number, tokens, width), F32)],
        compiler_params=pltpu.CompilerParams(vmem_limit_bytes=VMEM),
        cost_estimate=pl.CostEstimate(
            flops=flops, bytes_accessed=number * heads * size * width * 2, transcendentals=0
        ),
        name="attend",
    )(*keys, bias, *w_outs, *mix, *waits)


def backward_kernel(
    rows_v,
    left_v,
    right_v,
    rows_a,
    left_a,
    right_a,
    bias,
    grad_v,
    grad_a,
    w_out_v,
    w_out_a,
    *rest,
):
    own_v, own_a, to_left, to_right = rest[-4:]
    group, tokens, triple = rows_v.shape
    size = triple // 3
    factor = size**-0.5
    both_bias = bias[...].reshape(2 * tokens, 6 * tokens)
    width = w_out_v.shape[-1]
    grads_out = [
        lax.dot_general(
            grad[...], w_out[...].reshape(group * size, width), NT, preferred_element_type=F32
        ).astype(BF16)
        for grad, w_out in ((grad_v, w_out_v), (grad_a, w_out_a))
    ]
    for head in range(group):
        keys, values = key_values(head, rows_v, left_v, right_v, rows_a, left_a, right_a)
        queries = jnp.concatenate([rows_v[head, :, :size], rows_a[head, :, :size]], 0)
        grad_out = jnp.concatenate([g[:, head * size : (head + 1) * size] for g in grads_out], 0)
        prob = soft(queries, keys, both_bias, factor)
        grad_prob = lax.dot_general(grad_out, values, NT, preferred_element_type=F32)
        center = jnp.sum(prob * grad_prob, -1, keepdims=True)
        dscore = (prob * (grad_prob - center) * factor).astype(BF16)
        dquery = jnp.dot(dscore, keys, preferred_element_type=F32)
        dkey = lax.dot_general(dscore, queries, TN, preferred_element_type=F32)
        dvalue = lax.dot_general(prob.astype(BF16), grad_out, TN, preferred_element_type=F32)
        for part, own in enumerate((own_v, own_a)):
            base = 3 * tokens * part
            middle = slice(base + tokens, base + 2 * tokens)
            own[head, :, :size] = dquery[part * tokens : (part + 1) * tokens]
            own[head, :, size : 2 * size] = dkey[middle]
            own[head, :, 2 * size :] = dvalue[middle]
            for target, start in ((to_left, base), (to_right, base + 2 * tokens)):
                target[part, head, :, :size] = dkey[start : start + tokens].astype(BF16)
                target[part, head, :, size:] = dvalue[start : start + tokens].astype(BF16)


def attend_back(keys, bias, grad_v, grad_a, w_out_v, w_out_a, first, heads, waits):
    size, width = w_out_v.shape[1:]
    tokens = keys[0].shape[1]
    group = 2 if heads % 2 == 0 and first % 2 == 0 else 1
    own = jax.ShapeDtypeStruct((heads, tokens, 3 * size), F32)
    sent = jax.ShapeDtypeStruct((2, heads, tokens, 2 * size), BF16)
    sent_block = pl.BlockSpec((2, group, tokens, 2 * size), lambda i: (0, i, 0, 0))
    flops = 4 * heads * tokens * size * (30 * tokens + width)
    return pl.pallas_call(
        backward_kernel,
        grid=(heads // group,),
        out_shape=(own, own, sent, sent),
        in_specs=[head_block(group, array, first) for array in keys]
        + [
            pl.BlockSpec(bias.shape, lambda i: (0, 0, 0)),
            pl.BlockSpec(grad_v.shape, lambda i: (0, 0)),
            pl.BlockSpec(grad_a.shape, lambda i: (0, 0)),
            head_block(group, w_out_v, first),
            head_block(group, w_out_a, first),
        ]
        + [pl.BlockSpec(memory_space=pl.ANY)] * len(waits),
        out_specs=(head_block(group, own), head_block(group, own), sent_block, sent_block),
        compiler_params=pltpu.CompilerParams(vmem_limit_bytes=VMEM),
        cost_estimate=pl.CostEstimate(
            flops=flops, bytes_accessed=2 * heads * size * width * 2, transcendentals=0
        ),
        name="attend_back",
    )(*keys, bias, grad_v, grad_a, w_out_v, w_out_a, *waits)


def assemble_kernel(own_v, own_a, first, second, *rest):
    size = own_v.shape[-1] // 3
    out = rest[-1]
    for part, own in enumerate((own_v, own_a)):
        out[part, :, :, :size] = own[:, :, :size].astype(BF16)
        out[part, :, :, size:] = (
            own[:, :, size:] + first[part].astype(F32) + second[part].astype(F32)
        ).astype(BF16)


def assemble(own_v, own_a, first, second, waits):
    vmem = pl.BlockSpec(memory_space=pltpu.VMEM)
    return pl.pallas_call(
        assemble_kernel,
        out_shape=jax.ShapeDtypeStruct((2,) + own_v.shape, BF16),
        in_specs=[vmem] * 4 + [pl.BlockSpec(memory_space=pl.ANY)] * len(waits),
        out_specs=vmem,
        compiler_params=pltpu.CompilerParams(vmem_limit_bytes=VMEM),
        name="assemble",
    )(own_v, own_a, first, second, *waits)


def advance_kernel(coef, mods, start, *refs, terms):
    now, normed = refs[-2:]
    value = start[...].astype(F32) + coef[0] * sum(ref[...].astype(F32) for ref in refs[:terms])
    now[...] = value
    inv_rms = lax.rsqrt(jnp.mean(value * value, -1, keepdims=True) + EPSILON)
    normed[...] = (value * inv_rms * mods[...]).astype(BF16)


def advance(coef, mods, start, sums, waits):
    vmem = pl.BlockSpec(memory_space=pltpu.VMEM)
    return pl.pallas_call(
        functools.partial(advance_kernel, terms=len(sums)),
        out_shape=(
            jax.ShapeDtypeStruct(start.shape, F32),
            jax.ShapeDtypeStruct(start.shape, BF16),
        ),
        in_specs=[pl.BlockSpec(memory_space=pltpu.SMEM)]
        + [vmem] * (2 + len(sums))
        + [pl.BlockSpec(memory_space=pl.ANY)] * len(waits),
        out_specs=(vmem, vmem),
        compiler_params=pltpu.CompilerParams(vmem_limit_bytes=VMEM),
        name="advance",
    )(coef, mods, start, *sums, *waits)


def turn_kernel(place, first, second, out):
    devices, _, rows, _ = out.shape
    for part, ref in enumerate((first, second)):
        turned = ref[...].T
        for device in range(devices):
            out[device ^ place[0], part] = turned[device * rows : (device + 1) * rows]


def turn(place, first, second):
    vmem = pl.BlockSpec(memory_space=pltpu.VMEM)
    devices = lax.axis_size("clip") * lax.axis_size("vid")
    tokens, width = first.shape
    return pl.pallas_call(
        turn_kernel,
        out_shape=jax.ShapeDtypeStruct((devices, 2, width // devices, tokens), BF16),
        in_specs=[pl.BlockSpec(memory_space=pltpu.SMEM), vmem, vmem],
        out_specs=vmem,
        compiler_params=pltpu.CompilerParams(vmem_limit_bytes=VMEM),
        name="turn",
    )(place, first, second)


def differ_kernel(place, coef, start, now, *refs, terms):
    diff, grads, columns = refs[-3:]
    devices, _, wide = columns.shape
    value = start[...].astype(F32) - now[...]
    value = value + sum(ref[...].astype(F32) for ref in refs[:terms])
    diff[...] = value
    grad = (coef[0] * value).astype(BF16)
    grads[...] = grad
    for device in range(devices):
        columns[device ^ place[0]] = grad[:, device * wide : (device + 1) * wide]


def differ(place, coef, start, now, sums, waits):
    vmem = pl.BlockSpec(memory_space=pltpu.VMEM)
    smem = pl.BlockSpec(memory_space=pltpu.SMEM)
    devices = lax.axis_size("clip") * lax.axis_size("vid")
    tokens, width = start.shape
    return pl.pallas_call(
        functools.partial(differ_kernel, terms=len(sums)),
        out_shape=(
            jax.ShapeDtypeStruct((tokens, width), F32),
            jax.ShapeDtypeStruct((tokens, width), BF16),
            jax.ShapeDtypeStruct((devices, tokens, width // devices), BF16),
        ),
        in_specs=[smem, smem]
        + [vmem] * (2 + len(sums))
        + [pl.BlockSpec(memory_space=pl.ANY)] * len(waits),
        out_specs=(vmem,) * 3,
        compiler_params=pltpu.CompilerParams(vmem_limit_bytes=VMEM),
        name="differ",
    )(place, coef, start, now, *sums, *waits)


def weight_kernel(turned, *refs, parts, order):
    keep, send = refs[-2:]
    rows = keep.shape[1]
    blocks = []
    for ref in refs[:parts]:
        blocks += [ref[source, 0, 0] for source in range(ref.shape[0])]
    left = [
        jnp.concatenate([turned[source, late, 0] for source in order], 1) for late in range(2)
    ]
    result = jnp.dot(
        jnp.concatenate(left, 0), jnp.concatenate(blocks, 0), preferred_element_type=F32
    )
    keep[0] = result[:rows]
    send[0] = result[rows:].astype(BF16)


def weight_terms(turned, part, parts, order, waits):
    heads, tokens, width = parts[0].shape[2:]
    sources, late, _, rows, _ = turned.shape
    block = pl.BlockSpec((1, rows, width), lambda i: (i, 0, 0))
    return pl.pallas_call(
        functools.partial(weight_kernel, parts=len(parts), order=order),
        grid=(heads,),
        out_shape=(
            jax.ShapeDtypeStruct((heads, rows, width), F32),
            jax.ShapeDtypeStruct((heads, rows, width), BF16),
        ),
        in_specs=[pl.BlockSpec((sources, late, 1, rows, tokens), lambda i: (0, 0, part, 0, 0))]
        + [
            pl.BlockSpec((piece.shape[0], 1, 1, tokens, width), lambda i: (0, part, i, 0, 0))
            for piece in parts
        ]
        + [pl.BlockSpec(memory_space=pl.ANY)] * len(waits),
        out_specs=(block, block),
        compiler_params=pltpu.CompilerParams(vmem_limit_bytes=VMEM),
        name="weight_terms",
    )(turned, *parts, *waits)


def out_kernel(grads, *refs):
    keep, send = refs[-2:]
    wide = keep.shape[-1]
    heads_out = jnp.concatenate([ref[0, 0] for ref in refs[:-2]], 1)
    right = jnp.concatenate(
        [
            jnp.concatenate([grads[source, late] for late in range(2)], 1)
            for source in range(grads.shape[0])
        ],
        0,
    )
    result = jnp.dot(heads_out, right, preferred_element_type=F32)
    keep[0] = result[:, :wide]
    send[0] = result[:, wide:].astype(BF16)


def out_terms(grads, pieces, part):
    _, heads, size, tokens = pieces[0].shape
    wide = grads.shape[-1]
    block = pl.BlockSpec((1, size, wide), lambda i: (i, 0, 0))
    return pl.pallas_call(
        out_kernel,
        grid=(heads,),
        out_shape=(
            jax.ShapeDtypeStruct((heads, size, wide), F32),
            jax.ShapeDtypeStruct((heads, size, wide), BF16),
        ),
        in_specs=[pl.BlockSpec(grads.shape, lambda i: (0, 0, 0, 0))]
        + [pl.BlockSpec((1, 1, size, tokens), lambda i: (part, i, 0, 0))] * len(pieces),
        out_specs=(block, block),
        compiler_params=pltpu.CompilerParams(vmem_limit_bytes=VMEM),
        name="out_terms",
    )(grads, *pieces)


def project(normed, weight):
    return jnp.einsum("nd,dhe->hne", normed, weight, preferred_element_type=F32).astype(BF16)


def inverse_rms(current):
    return lax.rsqrt(jnp.mean(current * current, -1, keepdims=True) + EPSILON)


def norm_back(current, inv_rms, modulation, grad_normed):
    scaled = grad_normed * modulation
    return inv_rms * scaled - current * inv_rms**3 * jnp.mean(scaled * current, -1, keepdims=True)


def local(
    video_tokens,
    audio_tokens,
    qkv_video,
    out_video,
    qkv_audio,
    out_audio,
    gain_video,
    gain_audio,
    time_from,
    time_to,
    time_steps,
    windows,
    intersection,
):
    tokens = video_tokens.shape[1]
    size = out_video.shape[1]
    bias, mods = prepare(
        time_steps, windows, intersection, time_from, time_to, gain_video, gain_audio, tokens
    )

    def normalise(current, inv_rms, row):
        return (current * inv_rms * mods[row : row + 1]).astype(BF16)

    def widen(normed, weight):
        rows = project(normed, weight)
        sent = rows[:, :, size:]
        return [rows, shift(sent, "vid", 1), shift(sent, "vid", -1)]

    start_v = video_tokens[0].astype(F32)
    start_a = audio_tokens[0].astype(F32)
    inv_v, inv_a = inverse_rms(start_v), inverse_rms(start_a)
    stride = time_steps[0, 1].astype(F32)
    euler_step = -stride / TGRID
    span = -(STEPS * stride) / TGRID
    near, far = gather_steps(True), gather_steps(False)
    heads = out_video.shape[0]

    normed_v = normalise(start_v, inv_v, 2 * STEPS)
    normed_a = normalise(start_a, inv_a, 2 * STEPS + 1)
    place = lax.axis_index(("clip", "vid"))[None].astype(jnp.int32)
    dims = device_dims()
    now_v, now_a = video_tokens[0], audio_tokens[0]
    for step in range(STEPS):
        first, last = step == 0, step == STEPS - 1
        if first:
            keys = widen(normalise(start_v, inv_v, 0), qkv_video)
            keys += widen(normalise(start_a, inv_a, 1), qkv_audio)
        else:
            keys = widen(next_v, qkv_video)
            now_a, next_a = advance(
                euler_step[None], mods[row + 1 : row + 2], now_a, sums_a, (keys[0],)
            )
            keys += widen(next_a, qkv_audio)
        if first:
            student = widen(after(normed_v, keys[0], keys[3]), qkv_video)
            waits = ((student[0],), tuple(student[1:3]))
        else:
            waits = ((), ())
        if last:
            turned = turn(place, normed_v, after(normed_a, keys[0]))
            norm_stages = scatter_parts(turned.reshape(dims + turned.shape[1:]), far)
            norm_parts = norm_stages[-1]
            waits = ((), (norm_stages[0],))
            student_heads, student_field = attend(
                student,
                bias,
                (out_video, out_audio),
                (0, 1),
                F32,
                waits=(keys[3],),
                turned=True,
            )
            pieces = gather_list(student_heads, far)
        mix = (jnp.stack([span, -euler_step]), student_field) if last else ()
        _, field_v = attend(keys, bias, (out_video,), (0,), mix=mix, waits=waits[0])
        sums_v = exchange_groups(field_v[0])
        _, field_a = attend(keys, bias, (out_audio,), (1,), mix=mix, waits=(field_v,) + waits[1])
        sums_a = exchange_groups(field_a[0])
        if first:
            student += widen(after(normed_a, field_a), qkv_audio)
        if not last:
            row = 2 * step + 2
            now_v, next_v = advance(
                euler_step[None], mods[row : row + 1], now_v, sums_v, (student[3],)
            )
    diff_v, grad_v, columns = differ(
        place, span[None], video_tokens[0], now_v, sums_v, (*pieces[1:2], norm_stages[1])
    )
    stages_v = scatter_parts(columns.reshape(dims + columns.shape[1:]), far)
    diff_a, grad_a, columns = differ(
        place, span[None], audio_tokens[0], now_a, sums_a, (*pieces[2:4], stages_v[0])
    )
    stages_a = scatter_parts(columns.reshape(dims + columns.shape[1:]), far)

    halves = 2 if heads % 4 == 0 else 1
    count = heads // halves
    backs = []
    for half in range(halves):
        backs.append(
            attend_back(
                student,
                bias,
                grad_v,
                grad_a,
                out_video,
                out_audio,
                half * count,
                count,
                (backs[-1][2], *pieces[4:], norm_parts, stages_v[1], stages_a[0]) if half > 0 else (),
            )
        )
    out_v = out_terms(stages_v[-1], pieces, 0)
    out_a = out_terms(stages_a[-1], pieces, 1)
    chunks = []
    for half, (own_v, own_a, to_left, to_right) in enumerate(backs):
        waits = (backs[-1][2],) if half == 0 else (out_v[1],)
        chunks.append(
            assemble(own_v, own_a, shift(to_left, "vid", -1), shift(to_right, "vid", 1), waits)
        )

    out_came_v = swap(out_v[1], "clip", LATE_BIT)
    out_came_a = swap(out_a[1], "clip", LATE_BIT)

    terms = []
    line = {}

    def in_line(block, *key):
        line[key] = swap(after(block, line[key]) if key in line else block, *key)
        return line[key]

    backs = []
    for part in range(2):
        backs.append(jnp.concatenate([chunk[part] for chunk in chunks], 0))
    held = [((chunks[-1], stages_a[1]), (out_a[1], out_came_v))]
    early = {}
    for index, (chunk, steps) in enumerate(zip(chunks, (near, far))):
        blocks = [chunk]
        for level, step in enumerate(steps[:-1]):
            if level > 0:
                blocks[1] = after(blocks[1], *held[-1][0])
            done = early.get((index, step), [])
            blocks = blocks + done + [in_line(block, *step) for block in blocks[len(done) :]]
        if index == 0 and len(chunks) > 1:
            early[1, near[0]] = [in_line(after(chunks[1], stages_a[1]), *near[0])]
        blocks[-1] = after(blocks[-1], *held[-1][1], *early.get((index + 1, near[0]), []))
        parts = [jnp.stack(blocks)]
        for axis, bit in steps[-1:]:
            parts.append(swap(parts[0], axis, bit))
        both = []
        for part in range(2):
            keep, send = weight_terms(
                norm_parts,
                part,
                parts,
                source_order(steps, far),
                (both[0][1],) if part else (),
            )
            both.append((keep, send, swap(send, "clip", LATE_BIT)))
        terms.append(both)
        if index == 0:
            backs = [
                jnp.einsum(
                    "hne,dhe->nd", after(dqkv, both[1][1]), weight, preferred_element_type=F32
                ).astype(BF16)
                for dqkv, weight in zip(backs, (qkv_video, qkv_audio))
            ]
        held.append(((both[1][1],), (both[0][2], both[1][2], out_came_a, *backs)))

    final = terms[-1][1][1]
    w_out = [
        after(keep, final) + came.astype(F32)
        for keep, came in ((out_v[0], out_came_v), (out_a[0], out_came_a))
    ]
    results = []
    for part, (start, inv, row, diff) in enumerate(
        (
            (start_v, inv_v, 2 * STEPS, diff_v),
            (start_a, inv_a, 2 * STEPS + 1, diff_a),
        )
    ):
        back = sum(
            after(partial, final).astype(F32) for partial in exchange_groups(backs[part])
        )
        diff = after(diff, final)
        d_tokens = (diff + norm_back(start, inv, mods[row : row + 1], back)).astype(BF16)
        grad_qkv = jnp.concatenate(
            [after(both[part][0], final) + both[part][2].astype(F32) for both in terms], 0
        ).transpose(1, 0, 2)
        results.append((d_tokens[None], grad_qkv, w_out[part]))
    (d_video, wqkv_v, wout_v), (d_audio, wqkv_a, wout_a) = results
    return (d_video, d_audio, wqkv_v, wout_v, wqkv_a, wout_a)


def solution(mesh):
    return jax.shard_map(
        local,
        mesh=mesh,
        in_specs=(
            P("clip", "vid", None),
            P("clip", "vid", None),
            P(None, "aud", None),
            P("aud", None, None),
            P(None, "aud", None),
            P("aud", None, None),
            P(),
            P(),
            P(),
            P(),
            P("clip", None),
            P("clip", None),
            P("clip", None, None),
        ),
        out_specs=(
            P("clip", "vid", None),
            P("clip", "vid", None),
            P(("clip", "vid"), "aud", None),
            P("aud", None, ("clip", "vid")),
            P(("clip", "vid"), "aud", None),
            P("aud", None, ("clip", "vid")),
        ),
        check_vma=False,
    )
```

```python
import functools

import jax
import jax.numpy as jnp
from jax import lax
from jax.experimental import pallas as pl
from jax.experimental.pallas import tpu as pltpu
from jax.sharding import PartitionSpec as P

BLK = 32
TGRID = 64
STEPS = 2
EPSILON = 1e-06
MASKED = -1e30
F32 = jnp.float32
BF16 = jnp.bfloat16
NT = (((1,), (1,)), ((), ()))
TN = (((0,), (0,)), ((), ()))
VMEM = 48 * 2**20


def swap(block, axis, bit):
    count = lax.axis_size(axis)
    return lax.ppermute(block, axis, [(i, i ^ (1 << bit)) for i in range(count)])


def shift(block, axis, distance):
    count = lax.axis_size(axis)
    route = [(i, i + distance) for i in range(count) if 0 <= i + distance < count]
    return lax.ppermute(block, axis, route)


def bits_of(count):
    return count.bit_length() - 1


def after(block, *first):
    return lax.optimization_barrier((block, first))[0]


def gather_steps(near_first):
    clip = [("clip", 0)] if lax.axis_size("clip") > 1 else []
    vid = [("vid", bit) for bit in reversed(range(bits_of(lax.axis_size("vid"))))]
    return clip + vid if near_first else vid[:-1] + clip + vid[-1:]


def gather_list(block, steps):
    blocks = [block]
    for axis, bit in steps:
        blocks = blocks + [swap(part, axis, bit) for part in blocks]
    return blocks


def scatter_parts(parts, steps):
    left = gather_steps(True)
    parts = parts[None]
    stages = []
    for axis, bit in steps:
        place = 2 + left.index((axis, bit))
        left.remove((axis, bit))
        keep = lax.index_in_dim(parts, 0, place, keepdims=False)
        send = lax.index_in_dim(parts, 1, place, keepdims=False)
        parts = jnp.concatenate([keep, swap(send, axis, bit)], 0)
        stages.append(parts)
    return stages


def source_order(wanted, held):
    return [
        sum((i >> b & 1) << held.index(step) for b, step in enumerate(wanted))
        for i in range(1 << len(wanted))
    ]


def device_dims():
    steps = gather_steps(True)
    devices = lax.axis_size("clip") * lax.axis_size("vid")
    return (devices >> len(steps),) + (2,) * len(steps)


LATE_BIT = 1


def exchange_groups(partial):
    count = lax.axis_size("aud")
    return [partial] + [
        lax.ppermute(partial, "aud", [(i, i ^ step) for i in range(count)])
        for step in range(1, count)
    ]


def prepare_kernel(
    steps, place, windows, lists, time_from, time_to, gain_v, gain_a, bias, mods, *, tokens
):
    time_now, stride = steps[0], steps[1]
    levels = [(time_now, time_now), (time_now - stride, time_now - stride)]
    levels.append((time_now, time_now - STEPS * stride))
    for row, (start, end) in enumerate(levels):
        condition = time_from[pl.ds(start, 1), :] + time_to[pl.ds(end, 1), :]
        mods[2 * row : 2 * row + 1, :] = gain_v[...] * (1.0 + condition)
        mods[2 * row + 1 : 2 * row + 2, :] = gain_a[...] * (1.0 + condition)

    device = place[0]
    blocks = tokens // BLK
    all_blocks = place[1]
    shape = (tokens, 3 * tokens)
    row_pos = device * tokens + lax.broadcasted_iota(jnp.int32, shape, 0)
    column = lax.broadcasted_iota(jnp.int32, shape, 1)
    column_pos = (device - 1) * tokens + column
    inside = (column_pos >= 0) & (column_pos < all_blocks * BLK)
    distance = jnp.abs(row_pos - column_pos)
    row_blk = device * blocks + lax.broadcasted_iota(jnp.int32, shape, 0) // BLK
    column_blk = (device - 1) * blocks + column // BLK

    def fill(admitted, part, side):
        bias[part, :, side * 3 * tokens : (side + 1) * 3 * tokens] = jnp.where(
            admitted, 0.0, MASKED
        ).astype(F32)

    fill(inside & (distance < windows[0]), 0, 0)
    fill(inside & (distance < windows[1]), 1, 1)
    low = jnp.zeros(shape, jnp.int32)
    high = jnp.zeros(shape, jnp.int32)
    for block in range(blocks):
        here = row_blk == device * blocks + block
        low = jnp.where(here, lists[device * blocks + block, 0], low)
        high = jnp.where(here, lists[device * blocks + block, 1], high)
    fill(inside & (column_blk >= low) & (column_blk < high), 0, 1)
    low = jnp.zeros(shape, jnp.int32)
    high = jnp.zeros(shape, jnp.int32)
    for block in range(3 * blocks):
        index = (device - 1) * blocks + block
        safe = jnp.clip(index, 0, all_blocks - 1)
        here = column_blk == index
        low = jnp.where(here, lists[safe, 0], low)
        high = jnp.where(here, lists[safe, 1], high)
    fill(inside & (row_blk >= low) & (row_blk < high), 1, 0)


def prepare(time_steps, windows, intersection, time_from, time_to, gain_video, gain_audio, tokens):
    place = jnp.stack([lax.axis_index("vid"), lax.axis_size("vid") * tokens // BLK])
    smem = pl.BlockSpec(memory_space=pltpu.SMEM)
    vmem = pl.BlockSpec(memory_space=pltpu.VMEM)
    width = gain_video.shape[0]
    return pl.pallas_call(
        functools.partial(prepare_kernel, tokens=tokens),
        out_shape=(
            jax.ShapeDtypeStruct((2, tokens, 6 * tokens), F32),
            jax.ShapeDtypeStruct((6, width), F32),
        ),
        in_specs=[smem] * 4 + [vmem] * 4,
        out_specs=(vmem, vmem),
        name="prepare",
    )(
        time_steps[0],
        place.astype(jnp.int32),
        windows[0],
        intersection[0],
        time_from,
        time_to,
        gain_video[None],
        gain_audio[None],
    )


def soft(queries, keys, bias, factor):
    scores = lax.dot_general(queries, keys, NT, preferred_element_type=F32) * factor + bias
    shifted = jnp.exp(scores - jnp.max(scores, -1, keepdims=True))
    return shifted * (1.0 / jnp.sum(shifted, -1, keepdims=True))


def key_values(head, rows_v, left_v, right_v, rows_a, left_a, right_a):
    size = left_v.shape[-1] // 2
    keys, values = [], []
    for left, rows, right in ((left_v, rows_v, right_v), (left_a, rows_a, right_a)):
        keys += [left[head, :, :size], rows[head, :, size : 2 * size], right[head, :, :size]]
        values += [left[head, :, size:], rows[head, :, 2 * size :], right[head, :, size:]]
    return jnp.concatenate(keys, 0), jnp.concatenate(values, 0)


def forward_kernel(*refs, parts, mixed, waits, turned):
    rows_v, left_v, right_v, rows_a, left_a, right_a, bias = refs[:7]
    w_outs = refs[7 : 7 + len(parts)]
    at = 7 + len(parts)
    coef, other = refs[at : at + 2] if mixed else (None, None)
    heads_out, field, total = refs[at + 2 * mixed + waits :]
    step = pl.program_id(0)
    group, tokens, size = rows_v.shape[0], rows_v.shape[1], left_v.shape[-1] // 2
    outs = [[] for _ in parts]
    for head in range(group):
        keys, values = key_values(head, rows_v, left_v, right_v, rows_a, left_a, right_a)
        queries = jnp.concatenate([(rows_v, rows_a)[part][head, :, :size] for part in parts], 0)
        prob = soft(queries, keys, bias[...].reshape(-1, bias.shape[-1]), size**-0.5)
        out = jnp.dot(prob.astype(BF16), values, preferred_element_type=F32).astype(BF16)
        for index in range(len(parts)):
            outs[index].append(out[index * tokens : (index + 1) * tokens])
            heads_out[index, head] = outs[index][-1].T if turned else outs[index][-1]
    for index, w_out in enumerate(w_outs):
        term = jnp.dot(
            jnp.concatenate(outs[index], 1),
            w_out[...].reshape(group * size, w_out.shape[-1]),
            preferred_element_type=F32,
        )
        total[index] = jnp.where(step == 0, 0.0, total[index]) + term

    @pl.when(step == pl.num_programs(0) - 1)
    def _():
        result = total[...]
        if mixed:
            result = coef[0] * other[...] + coef[1] * result
        field[...] = result.astype(field.dtype)


def head_block(group, array, first=0):
    return pl.BlockSpec((group,) + array.shape[1:], lambda i: (i + first // group, 0, 0))


def attend(keys, bias, w_outs, parts, dtype=BF16, mix=(), waits=(), turned=False):
    heads, size, width = w_outs[0].shape
    tokens = keys[0].shape[1]
    group = 2 if heads % 2 == 0 else 1
    number = len(parts)
    out_dims = (size, tokens) if turned else (tokens, size)
    flops = 2 * number * heads * tokens * size * (12 * tokens + width)
    whole = pl.BlockSpec((number, tokens, width), lambda i: (0, 0, 0))
    one = pl.BlockSpec((1, tokens, width), lambda i: (parts[0], 0, 0))
    return pl.pallas_call(
        functools.partial(forward_kernel, parts=parts, mixed=bool(mix), waits=len(waits), turned=turned),
        grid=(heads // group,),
        out_shape=(
            jax.ShapeDtypeStruct((number, heads) + out_dims, BF16),
            jax.ShapeDtypeStruct((number, tokens, width), dtype),
        ),
        in_specs=[head_block(group, array) for array in keys]
        + [pl.BlockSpec((number,) + bias.shape[1:], lambda i: (parts[0], 0, 0))]
        + [head_block(group, w_out) for w_out in w_outs]
        + ([pl.BlockSpec(memory_space=pltpu.SMEM), one] if mix else [])
        + [pl.BlockSpec(memory_space=pl.ANY)] * len(waits),
        out_specs=(
            pl.BlockSpec((number, group) + out_dims, lambda i: (0, i, 0, 0)),
            whole,
        ),
        scratch_shapes=[pltpu.VMEM((number, tokens, width), F32)],
        compiler_params=pltpu.CompilerParams(vmem_limit_bytes=VMEM),
        cost_estimate=pl.CostEstimate(
            flops=flops, bytes_accessed=number * heads * size * width * 2, transcendentals=0
        ),
        name="attend",
    )(*keys, bias, *w_outs, *mix, *waits)


def backward_kernel(
    rows_v,
    left_v,
    right_v,
    rows_a,
    left_a,
    right_a,
    bias,
    grad_v,
    grad_a,
    w_out_v,
    w_out_a,
    *rest,
):
    own_v, own_a, to_left, to_right = rest[-4:]
    group, tokens, triple = rows_v.shape
    size = triple // 3
    factor = size**-0.5
    both_bias = bias[...].reshape(2 * tokens, 6 * tokens)
    width = w_out_v.shape[-1]
    grads_out = [
        lax.dot_general(
            grad[...], w_out[...].reshape(group * size, width), NT, preferred_element_type=F32
        ).astype(BF16)
        for grad, w_out in ((grad_v, w_out_v), (grad_a, w_out_a))
    ]
    for head in range(group):
        keys, values = key_values(head, rows_v, left_v, right_v, rows_a, left_a, right_a)
        queries = jnp.concatenate([rows_v[head, :, :size], rows_a[head, :, :size]], 0)
        grad_out = jnp.concatenate([g[:, head * size : (head + 1) * size] for g in grads_out], 0)
        prob = soft(queries, keys, both_bias, factor)
        grad_prob = lax.dot_general(grad_out, values, NT, preferred_element_type=F32)
        center = jnp.sum(prob * grad_prob, -1, keepdims=True)
        dscore = (prob * (grad_prob - center) * factor).astype(BF16)
        dquery = jnp.dot(dscore, keys, preferred_element_type=F32)
        dkey = lax.dot_general(dscore, queries, TN, preferred_element_type=F32)
        dvalue = lax.dot_general(prob.astype(BF16), grad_out, TN, preferred_element_type=F32)
        for part, own in enumerate((own_v, own_a)):
            base = 3 * tokens * part
            middle = slice(base + tokens, base + 2 * tokens)
            own[head, :, :size] = dquery[part * tokens : (part + 1) * tokens]
            own[head, :, size : 2 * size] = dkey[middle]
            own[head, :, 2 * size :] = dvalue[middle]
            for target, start in ((to_left, base), (to_right, base + 2 * tokens)):
                target[part, head, :, :size] = dkey[start : start + tokens].astype(BF16)
                target[part, head, :, size:] = dvalue[start : start + tokens].astype(BF16)


def attend_back(keys, bias, grad_v, grad_a, w_out_v, w_out_a, first, heads, waits):
    size, width = w_out_v.shape[1:]
    tokens = keys[0].shape[1]
    group = 2 if heads % 2 == 0 and first % 2 == 0 else 1
    own = jax.ShapeDtypeStruct((heads, tokens, 3 * size), F32)
    sent = jax.ShapeDtypeStruct((2, heads, tokens, 2 * size), BF16)
    sent_block = pl.BlockSpec((2, group, tokens, 2 * size), lambda i: (0, i, 0, 0))
    flops = 4 * heads * tokens * size * (30 * tokens + width)
    return pl.pallas_call(
        backward_kernel,
        grid=(heads // group,),
        out_shape=(own, own, sent, sent),
        in_specs=[head_block(group, array, first) for array in keys]
        + [
            pl.BlockSpec(bias.shape, lambda i: (0, 0, 0)),
            pl.BlockSpec(grad_v.shape, lambda i: (0, 0)),
            pl.BlockSpec(grad_a.shape, lambda i: (0, 0)),
            head_block(group, w_out_v, first),
            head_block(group, w_out_a, first),
        ]
        + [pl.BlockSpec(memory_space=pl.ANY)] * len(waits),
        out_specs=(head_block(group, own), head_block(group, own), sent_block, sent_block),
        compiler_params=pltpu.CompilerParams(vmem_limit_bytes=VMEM),
        cost_estimate=pl.CostEstimate(
            flops=flops, bytes_accessed=2 * heads * size * width * 2, transcendentals=0
        ),
        name="attend_back",
    )(*keys, bias, grad_v, grad_a, w_out_v, w_out_a, *waits)


def assemble_kernel(own_v, own_a, first, second, *rest):
    size = own_v.shape[-1] // 3
    out = rest[-1]
    for part, own in enumerate((own_v, own_a)):
        out[part, :, :, :size] = own[:, :, :size].astype(BF16)
        out[part, :, :, size:] = (
            own[:, :, size:] + first[part].astype(F32) + second[part].astype(F32)
        ).astype(BF16)


def assemble(own_v, own_a, first, second, waits):
    vmem = pl.BlockSpec(memory_space=pltpu.VMEM)
    return pl.pallas_call(
        assemble_kernel,
        out_shape=jax.ShapeDtypeStruct((2,) + own_v.shape, BF16),
        in_specs=[vmem] * 4 + [pl.BlockSpec(memory_space=pl.ANY)] * len(waits),
        out_specs=vmem,
        compiler_params=pltpu.CompilerParams(vmem_limit_bytes=VMEM),
        name="assemble",
    )(own_v, own_a, first, second, *waits)


def advance_kernel(coef, mods, start, *refs, terms):
    now, normed = refs[-2:]
    value = start[...].astype(F32) + coef[0] * sum(ref[...].astype(F32) for ref in refs[:terms])
    now[...] = value
    inv_rms = lax.rsqrt(jnp.mean(value * value, -1, keepdims=True) + EPSILON)
    normed[...] = (value * inv_rms * mods[...]).astype(BF16)


def advance(coef, mods, start, sums, waits):
    vmem = pl.BlockSpec(memory_space=pltpu.VMEM)
    return pl.pallas_call(
        functools.partial(advance_kernel, terms=len(sums)),
        out_shape=(
            jax.ShapeDtypeStruct(start.shape, F32),
            jax.ShapeDtypeStruct(start.shape, BF16),
        ),
        in_specs=[pl.BlockSpec(memory_space=pltpu.SMEM)]
        + [vmem] * (2 + len(sums))
        + [pl.BlockSpec(memory_space=pl.ANY)] * len(waits),
        out_specs=(vmem, vmem),
        compiler_params=pltpu.CompilerParams(vmem_limit_bytes=VMEM),
        name="advance",
    )(coef, mods, start, *sums, *waits)


def turn_kernel(place, first, second, out):
    devices, _, rows, _ = out.shape
    for part, ref in enumerate((first, second)):
        turned = ref[...].T
        for device in range(devices):
            out[device ^ place[0], part] = turned[device * rows : (device + 1) * rows]


def turn(place, first, second):
    vmem = pl.BlockSpec(memory_space=pltpu.VMEM)
    devices = lax.axis_size("clip") * lax.axis_size("vid")
    tokens, width = first.shape
    return pl.pallas_call(
        turn_kernel,
        out_shape=jax.ShapeDtypeStruct((devices, 2, width // devices, tokens), BF16),
        in_specs=[pl.BlockSpec(memory_space=pltpu.SMEM), vmem, vmem],
        out_specs=vmem,
        compiler_params=pltpu.CompilerParams(vmem_limit_bytes=VMEM),
        name="turn",
    )(place, first, second)


def differ_kernel(place, coef, start, now, *refs, terms):
    diff, grads, columns = refs[-3:]
    devices, _, wide = columns.shape
    value = start[...].astype(F32) - now[...]
    value = value + sum(ref[...].astype(F32) for ref in refs[:terms])
    diff[...] = value
    grad = (coef[0] * value).astype(BF16)
    grads[...] = grad
    for device in range(devices):
        columns[device ^ place[0]] = grad[:, device * wide : (device + 1) * wide]


def differ(place, coef, start, now, sums, waits):
    vmem = pl.BlockSpec(memory_space=pltpu.VMEM)
    smem = pl.BlockSpec(memory_space=pltpu.SMEM)
    devices = lax.axis_size("clip") * lax.axis_size("vid")
    tokens, width = start.shape
    return pl.pallas_call(
        functools.partial(differ_kernel, terms=len(sums)),
        out_shape=(
            jax.ShapeDtypeStruct((tokens, width), F32),
            jax.ShapeDtypeStruct((tokens, width), BF16),
            jax.ShapeDtypeStruct((devices, tokens, width // devices), BF16),
        ),
        in_specs=[smem, smem]
        + [vmem] * (2 + len(sums))
        + [pl.BlockSpec(memory_space=pl.ANY)] * len(waits),
        out_specs=(vmem,) * 3,
        compiler_params=pltpu.CompilerParams(vmem_limit_bytes=VMEM),
        name="differ",
    )(place, coef, start, now, *sums, *waits)


def weight_kernel(turned, *refs, parts, order):
    keep, send = refs[-2:]
    rows = keep.shape[1]
    blocks = []
    for ref in refs[:parts]:
        blocks += [ref[source, 0, 0] for source in range(ref.shape[0])]
    left = [
        jnp.concatenate([turned[source, late, 0] for source in order], 1) for late in range(2)
    ]
    result = jnp.dot(
        jnp.concatenate(left, 0), jnp.concatenate(blocks, 0), preferred_element_type=F32
    )
    keep[0] = result[:rows]
    send[0] = result[rows:].astype(BF16)


def weight_terms(turned, part, parts, order, waits):
    heads, tokens, width = parts[0].shape[2:]
    sources, late, _, rows, _ = turned.shape
    block = pl.BlockSpec((1, rows, width), lambda i: (i, 0, 0))
    return pl.pallas_call(
        functools.partial(weight_kernel, parts=len(parts), order=order),
        grid=(heads,),
        out_shape=(
            jax.ShapeDtypeStruct((heads, rows, width), F32),
            jax.ShapeDtypeStruct((heads, rows, width), BF16),
        ),
        in_specs=[pl.BlockSpec((sources, late, 1, rows, tokens), lambda i: (0, 0, part, 0, 0))]
        + [
            pl.BlockSpec((piece.shape[0], 1, 1, tokens, width), lambda i: (0, part, i, 0, 0))
            for piece in parts
        ]
        + [pl.BlockSpec(memory_space=pl.ANY)] * len(waits),
        out_specs=(block, block),
        compiler_params=pltpu.CompilerParams(vmem_limit_bytes=VMEM),
        name="weight_terms",
    )(turned, *parts, *waits)


def out_kernel(grads, *refs):
    keep, send = refs[-2:]
    wide = keep.shape[-1]
    heads_out = jnp.concatenate([ref[0, 0] for ref in refs[:-2]], 1)
    right = jnp.concatenate(
        [
            jnp.concatenate([grads[source, late] for late in range(2)], 1)
            for source in range(grads.shape[0])
        ],
        0,
    )
    result = jnp.dot(heads_out, right, preferred_element_type=F32)
    keep[0] = result[:, :wide]
    send[0] = result[:, wide:].astype(BF16)


def out_terms(grads, pieces, part):
    _, heads, size, tokens = pieces[0].shape
    wide = grads.shape[-1]
    block = pl.BlockSpec((1, size, wide), lambda i: (i, 0, 0))
    return pl.pallas_call(
        out_kernel,
        grid=(heads,),
        out_shape=(
            jax.ShapeDtypeStruct((heads, size, wide), F32),
            jax.ShapeDtypeStruct((heads, size, wide), BF16),
        ),
        in_specs=[pl.BlockSpec(grads.shape, lambda i: (0, 0, 0, 0))]
        + [pl.BlockSpec((1, 1, size, tokens), lambda i: (part, i, 0, 0))] * len(pieces),
        out_specs=(block, block),
        compiler_params=pltpu.CompilerParams(vmem_limit_bytes=VMEM),
        name="out_terms",
    )(grads, *pieces)


def project(normed, weight):
    return jnp.einsum("nd,dhe->hne", normed, weight, preferred_element_type=F32).astype(BF16)


def inverse_rms(current):
    return lax.rsqrt(jnp.mean(current * current, -1, keepdims=True) + EPSILON)


def norm_back(current, inv_rms, modulation, grad_normed):
    scaled = grad_normed * modulation
    return inv_rms * scaled - current * inv_rms**3 * jnp.mean(scaled * current, -1, keepdims=True)


def local(
    video_tokens,
    audio_tokens,
    qkv_video,
    out_video,
    qkv_audio,
    out_audio,
    gain_video,
    gain_audio,
    time_from,
    time_to,
    time_steps,
    windows,
    intersection,
):
    tokens = video_tokens.shape[1]
    size = out_video.shape[1]
    bias, mods = prepare(
        time_steps, windows, intersection, time_from, time_to, gain_video, gain_audio, tokens
    )

    def normalise(current, inv_rms, row):
        return (current * inv_rms * mods[row : row + 1]).astype(BF16)

    def widen(normed, weight):
        rows = project(normed, weight)
        sent = rows[:, :, size:]
        return [rows, shift(sent, "vid", 1), shift(sent, "vid", -1)]

    start_v = video_tokens[0].astype(F32)
    start_a = audio_tokens[0].astype(F32)
    inv_v, inv_a = inverse_rms(start_v), inverse_rms(start_a)
    stride = time_steps[0, 1].astype(F32)
    euler_step = -stride / TGRID
    span = -(STEPS * stride) / TGRID
    near, far = gather_steps(True), gather_steps(False)
    heads = out_video.shape[0]

    normed_v = normalise(start_v, inv_v, 2 * STEPS)
    normed_a = normalise(start_a, inv_a, 2 * STEPS + 1)
    place = lax.axis_index(("clip", "vid"))[None].astype(jnp.int32)
    dims = device_dims()
    now_v, now_a = video_tokens[0], audio_tokens[0]
    for step in range(STEPS):
        first, last = step == 0, step == STEPS - 1
        if first:
            keys = widen(normalise(start_v, inv_v, 0), qkv_video)
            keys += widen(normalise(start_a, inv_a, 1), qkv_audio)
        else:
            keys = widen(next_v, qkv_video)
            now_a, next_a = advance(
                euler_step[None], mods[row + 1 : row + 2], now_a, sums_a, (keys[0],)
            )
            keys += widen(next_a, qkv_audio)
        if first:
            student = widen(after(normed_v, keys[0], keys[3]), qkv_video)
            waits = ((student[0],), tuple(student[1:3]))
        else:
            waits = ((), ())
        if last:
            turned = turn(place, normed_v, after(normed_a, keys[0]))
            norm_stages = scatter_parts(turned.reshape(dims + turned.shape[1:]), far)
            norm_parts = norm_stages[-1]
            waits = ((), (norm_stages[0],))
            student_heads, student_field = attend(
                student,
                bias,
                (out_video, out_audio),
                (0, 1),
                F32,
                waits=(keys[3],),
                turned=True,
            )
            pieces = gather_list(student_heads, far)
        mix = (jnp.stack([span, -euler_step]), student_field) if last else ()
        _, field_v = attend(keys, bias, (out_video,), (0,), mix=mix, waits=waits[0])
        sums_v = exchange_groups(field_v[0])
        _, field_a = attend(keys, bias, (out_audio,), (1,), mix=mix, waits=(field_v,) + waits[1])
        sums_a = exchange_groups(field_a[0])
        if first:
            student += widen(after(normed_a, field_a), qkv_audio)
        if not last:
            row = 2 * step + 2
            now_v, next_v = advance(
                euler_step[None], mods[row : row + 1], now_v, sums_v, (student[3],)
            )
    diff_v, grad_v, columns = differ(
        place, span[None], video_tokens[0], now_v, sums_v, (*pieces[1:2], norm_stages[1])
    )
    stages_v = scatter_parts(columns.reshape(dims + columns.shape[1:]), far)
    diff_a, grad_a, columns = differ(
        place, span[None], audio_tokens[0], now_a, sums_a, (*pieces[2:4], stages_v[0])
    )
    stages_a = scatter_parts(columns.reshape(dims + columns.shape[1:]), far)

    halves = 2 if heads % 4 == 0 else 1
    count = heads // halves
    backs = []
    for half in range(halves):
        backs.append(
            attend_back(
                student,
                bias,
                grad_v,
                grad_a,
                out_video,
                out_audio,
                half * count,
                count,
                (backs[-1][2], *pieces[4:], norm_parts, stages_v[1], stages_a[0]) if half > 0 else (),
            )
        )
    out_v = out_terms(stages_v[-1], pieces, 0)
    out_a = out_terms(stages_a[-1], pieces, 1)
    chunks = []
    for half, (own_v, own_a, to_left, to_right) in enumerate(backs):
        waits = (backs[-1][2],) if half == 0 else (out_v[1],)
        chunks.append(
            assemble(own_v, own_a, shift(to_left, "vid", -1), shift(to_right, "vid", 1), waits)
        )

    out_came_v = swap(out_v[1], "clip", LATE_BIT)
    out_came_a = swap(out_a[1], "clip", LATE_BIT)

    terms = []
    line = {}

    def in_line(block, *key):
        line[key] = swap(after(block, line[key]) if key in line else block, *key)
        return line[key]

    backs = []
    for part in range(2):
        backs.append(jnp.concatenate([chunk[part] for chunk in chunks], 0))
    held = [((chunks[-1], stages_a[1]), (out_a[1], out_came_v))]
    early = {}
    for index, (chunk, steps) in enumerate(zip(chunks, (near, far))):
        blocks = [chunk]
        for level, step in enumerate(steps[:-1]):
            if level > 0:
                blocks[1] = after(blocks[1], *held[-1][0])
            done = early.get((index, step), [])
            blocks = blocks + done + [in_line(block, *step) for block in blocks[len(done) :]]
        if index == 0 and len(chunks) > 1:
            early[1, near[0]] = [in_line(after(chunks[1], stages_a[1]), *near[0])]
        blocks[-1] = after(blocks[-1], *held[-1][1], *early.get((index + 1, near[0]), []))
        parts = [jnp.stack(blocks)]
        for axis, bit in steps[-1:]:
            parts.append(swap(parts[0], axis, bit))
        both = []
        for part in range(2):
            keep, send = weight_terms(
                norm_parts,
                part,
                parts,
                source_order(steps, far),
                (both[0][1],) + (out_came_a,) * index if part else (),
            )
            both.append((keep, send, swap(send, "clip", LATE_BIT)))
        terms.append(both)
        if index == 0:
            backs = [
                jnp.einsum(
                    "hne,dhe->nd", after(dqkv, both[1][1]), weight, preferred_element_type=F32
                ).astype(BF16)
                for dqkv, weight in zip(backs, (qkv_video, qkv_audio))
            ]
        held.append(((both[1][1],), (both[0][2], both[1][2], *backs)))

    final = terms[-1][1][1]
    w_out = [
        after(keep, final) + came.astype(F32)
        for keep, came in ((out_v[0], out_came_v), (out_a[0], out_came_a))
    ]
    results = []
    for part, (start, inv, row, diff) in enumerate(
        (
            (start_v, inv_v, 2 * STEPS, diff_v),
            (start_a, inv_a, 2 * STEPS + 1, diff_a),
        )
    ):
        back = sum(
            after(partial, final).astype(F32) for partial in exchange_groups(backs[part])
        )
        diff = after(diff, final)
        d_tokens = (diff + norm_back(start, inv, mods[row : row + 1], back)).astype(BF16)
        grad_qkv = jnp.concatenate(
            [after(both[part][0], final) + both[part][2].astype(F32) for both in terms], 0
        ).transpose(1, 0, 2)
        results.append((d_tokens[None], grad_qkv, w_out[part]))
    (d_video, wqkv_v, wout_v), (d_audio, wqkv_a, wout_a) = results
    return (d_video, d_audio, wqkv_v, wout_v, wqkv_a, wout_a)


def solution(mesh):
    return jax.shard_map(
        local,
        mesh=mesh,
        in_specs=(
            P("clip", "vid", None),
            P("clip", "vid", None),
            P(None, "aud", None),
            P("aud", None, None),
            P(None, "aud", None),
            P("aud", None, None),
            P(),
            P(),
            P(),
            P(),
            P("clip", None),
            P("clip", None),
            P("clip", None, None),
        ),
        out_specs=(
            P("clip", "vid", None),
            P("clip", "vid", None),
            P(("clip", "vid"), "aud", None),
            P("aud", None, ("clip", "vid")),
            P(("clip", "vid"), "aud", None),
            P("aud", None, ("clip", "vid")),
        ),
        check_vma=False,
    )
```
